256 devices in a mesh: expert: 16 (over z, core), dp: 4 (over x), tensor: 4 (over y).
Axes of the slice: x: 4, y: 4, z: 8, core: 2. Of those that a mesh axis runs over, the one named last changes fastest.
Arguments:
- grad_out: bfloat16 [8192, 2048], P('expert', ('dp', 'tensor')), may hold values from -9 to 9
- gate_prob: float32 [8192], P('expert'), may hold values from 0.1 to 1
- expert_ids: int32 [8192], P('expert'), may hold values from 0 to 15, as said below
- slot_index: int32 [8192], P('expert'), may hold values from -1 to 39, as said below
- saved_rows: bfloat16 [16, 1280, 2048], P('expert', 'dp'), may hold values from -6 to 6
- row_rank: int32 [16, 16, 40], P('expert'), may hold values from -1 to 639, as said below
- part_counts: int32 [16, 4], P('expert'), may hold values from 0 to 320, as said below
- w_gate: bfloat16 [16, 2048, 4096], P('expert', None, ('dp', 'tensor')), may hold values from -0.125 to 0.125
- w_up: bfloat16 [16, 2048, 4096], P('expert', None, ('dp', 'tensor')), may hold values from -0.125 to 0.125
- w_down: bfloat16 [16, 4096, 2048], P('expert', ('dp', 'tensor')), may hold values from -0.09375 to 0.09375
Outputs:
- grad_input: bfloat16 [8192, 2048], P('expert', ('dp', 'tensor'))
- grad_gate: bfloat16 [16, 2048, 4096], P('expert', None, ('dp', 'tensor'))
- grad_up: bfloat16 [16, 2048, 4096], P('expert', None, ('dp', 'tensor'))
- grad_down: bfloat16 [16, 4096, 2048], P('expert', ('dp', 'tensor'))
The draws below stay inside these ranges and needn't reach their ends.
Inputs may be any that keep to these rules, and one draw needn't show every extreme that they name: `expert_ids`: in every draw one expert is chosen by 40 or more tokens of every group. `slot_index`: the number of earlier tokens of the same group with the same expert, or -1 once that number reaches 40. `row_rank`: -1 exactly where the slot holds no token (slot c of group s for expert e holds one when c < the number of tokens of group s with slot_index >= 0 and expert e); the slots of expert e that hold tokens take positions 0 to their number - 1, each once. part_counts[e] sums to the number of slots of expert e that hold tokens; expert e's compacted list lies in partition order, partition p holding its part_counts[e, p] positions in its first rows; in every draw some partition is full.
All inputs are finite; a program needn't handle non-finite values.
Results may differ from the reference program's by a relative error of at most 0.0057.
Values may be sent and summed in bfloat16 or wider, within the bound.
A program may use at most 64 MiB of HBM per device.

```python
import jax
import jax.numpy as jnp
from jax import lax

D = 2048
HID = 4096
TOK_GRP = 512
EXPERTS = 16
TOKENS = 8192
CAP = 40
ROWS = 640
KEEP_CAP = 320
N_DP = 4


def layout(key):
    subkeys = jax.random.split(key, 7)
    draw_one = jax.random.randint(subkeys[0], (EXPERTS, TOK_GRP), 0, EXPERTS)
    second = jax.random.randint(subkeys[1], (EXPERTS, TOK_GRP), 0, EXPERTS)
    expert_order = jax.random.permutation(subkeys[2], EXPERTS)
    raw_ids = expert_order[jnp.minimum(draw_one, second)]
    busiest = expert_order[0]
    places = jax.vmap(lambda sub: jax.random.permutation(sub, TOK_GRP))(jax.random.split(subkeys[3], EXPERTS))
    chosen = jnp.where(places < CAP, busiest, raw_ids).astype(jnp.int32)
    one_hot = (chosen[:, :, None] == jnp.arange(EXPERTS, dtype=jnp.int32)[None, None, :]).astype(jnp.int32)
    arrival = jnp.sum((jnp.cumsum(one_hot, axis=1) - 1) * one_hot, axis=2)
    slot_ids = jnp.where(arrival < CAP, arrival, -1).astype(jnp.int32)
    bin_loads = jnp.minimum(jnp.sum(one_hot, axis=1), CAP)
    slot_kept = jnp.arange(CAP, dtype=jnp.int32)[None, None, :] < bin_loads[:, :, None]
    kept_bins = jnp.transpose(slot_kept, (1, 0, 2))
    totals = jnp.sum(kept_bins.astype(jnp.int32), axis=(1, 2))
    priority = jax.vmap(lambda sub: jax.random.permutation(sub, ROWS))(jax.random.split(subkeys[4], EXPERTS))
    flat_kept = kept_bins.reshape(EXPERTS, ROWS)
    priority = jnp.where(flat_kept, priority, priority + ROWS).astype(jnp.int32)
    position = jnp.argsort(jnp.argsort(priority, axis=1), axis=1).astype(jnp.int32)
    positions = jnp.where(flat_kept, position, -1).astype(jnp.int32).reshape(EXPERTS, EXPERTS, CAP)
    lowest = (totals + N_DP - 1) // N_DP
    limit_rows = jax.random.randint(subkeys[5], (EXPERTS,), lowest, KEEP_CAP + 1)
    limit_rows = jnp.where(jnp.arange(EXPERTS) == busiest, KEEP_CAP, limit_rows).astype(jnp.int32)
    filled = jnp.clip(totals[:, None] - jnp.arange(N_DP, dtype=jnp.int32)[None, :] * limit_rows[:, None], 0, limit_rows[:, None])
    rotation = jax.random.randint(subkeys[6], (EXPERTS,), 0, N_DP)
    source = (jnp.arange(N_DP, dtype=jnp.int32)[None, :] - rotation[:, None]) % N_DP
    counts = jnp.take_along_axis(filled, source, axis=1).astype(jnp.int32)
    return (chosen.reshape(-1), slot_ids.reshape(-1), positions, counts)


def draw_expert_ids(key, part):
    shared = layout(key)
    return shared[0]


def draw_slot_index(key, part):
    shared = layout(key)
    return shared[1]


def draw_row_rank(key, part):
    shared = layout(key)
    return shared[2]


def draw_part_counts(key, part):
    shared = layout(key)
    return shared[3]


def steps_of(rng, shape, cuts, smallest, largest):
    loudness, own = 1.0, jax.random.fold_in(rng, 6)
    for dim, shards_of in cuts:
        heights = jnp.exp(jax.random.uniform(jax.random.fold_in(own, dim), (shards_of,), jnp.float32, smallest / len(cuts), largest / len(cuts)))
        loudness = loudness * jnp.repeat(heights, shape[dim] // shards_of).reshape([-1 if axis == dim else 1 for axis in range(len(shape))])
    return loudness


def noise(key, extent, spread, limit, cuts=(), kind=jnp.bfloat16):
    loudness = steps_of(key, extent, cuts, -0.22, 0.18) if cuts else 1.0
    array = jax.random.normal(key, extent, jnp.float32) * spread * loudness
    return jnp.minimum(jnp.maximum(array, -limit), limit).astype(kind)


def setup_inputs(seed: int = 0) -> dict:
    splits = jax.random.split(jax.random.key(seed), 11)
    return {
        "grad_out": noise(splits[0], (TOKENS, D), 1.5, 9.0, ((0, 16), (1, 16))),
        "gate_prob": jnp.clip(0.1 + 0.9 * jax.random.uniform(splits[1], (TOKENS,), jnp.float32) ** steps_of(splits[1], (TOKENS,), ((0, 16),), -0.2, 0.2), 0.1, 1.0),
        "expert_ids": draw_expert_ids(jax.random.fold_in(splits[10], 71), 0),
        "slot_index": draw_slot_index(jax.random.fold_in(splits[10], 71), 0),
        "saved_rows": noise(splits[4], (EXPERTS, N_DP * KEEP_CAP, D), 1.0, 6.0, ((0, 16), (1, 4))),
        "row_rank": draw_row_rank(jax.random.fold_in(splits[10], 71), 0),
        "part_counts": draw_part_counts(jax.random.fold_in(splits[10], 71), 0),
        "w_gate": noise(splits[7], (EXPERTS, D, HID), D ** -0.5, 0.125, ((0, 16), (2, 16))),
        "w_up": noise(splits[8], (EXPERTS, D, HID), D ** -0.5, 0.125, ((0, 16), (2, 16))),
        "w_down": noise(splits[9], (EXPERTS, HID, D), HID ** -0.5, 0.09375, ((0, 16), (1, 16))),
    }


def locate(positions, counts):
    bounds = jnp.cumsum(counts)
    partition = jnp.sum((positions[..., None] >= bounds).astype(jnp.int32), axis=-1)
    below_part = jnp.arange(counts.shape[0], dtype=jnp.int32) < partition[..., None]
    offsets = jnp.sum(jnp.where(below_part, counts, 0), axis=-1)
    slot_kept = positions >= 0
    row_index = jnp.where(slot_kept, partition * KEEP_CAP + positions - offsets, 0).astype(jnp.int32)
    return slot_kept, row_index


def expert_grads(inputs, grad_rows, gate_weight, up_weight, down_weight):
    gate_pre = jnp.dot(inputs, gate_weight, preferred_element_type=jnp.float32)
    up_pre = jnp.dot(inputs, up_weight, preferred_element_type=jnp.float32)
    squash = jax.nn.sigmoid(gate_pre)
    activated = gate_pre * squash
    hidden = (activated * up_pre).astype(jnp.bfloat16)
    hidden_grad = lax.dot_general(grad_rows, down_weight, (((1,), (1,)), ((), ())), preferred_element_type=jnp.float32)
    up_grad = (hidden_grad * activated).astype(jnp.bfloat16)
    gate_grad = (hidden_grad * up_pre * squash * (1.0 + gate_pre * (1.0 - squash))).astype(jnp.bfloat16)
    partial_value = lax.dot_general(gate_grad, gate_weight, (((1,), (1,)), ((), ())), preferred_element_type=jnp.float32)
    partial_value = partial_value + lax.dot_general(up_grad, up_weight, (((1,), (1,)), ((), ())), preferred_element_type=jnp.float32)
    gate_wgrad = lax.dot_general(inputs, gate_grad, (((0,), (0,)), ((), ())), preferred_element_type=jnp.float32)
    up_wgrad = lax.dot_general(inputs, up_grad, (((0,), (0,)), ((), ())), preferred_element_type=jnp.float32)
    down_wgrad = lax.dot_general(hidden, grad_rows, (((0,), (0,)), ((), ())), preferred_element_type=jnp.float32)
    return partial_value, gate_wgrad.astype(jnp.bfloat16), up_wgrad.astype(jnp.bfloat16), down_wgrad.astype(jnp.bfloat16)


def reference(grad_out, gate_prob, expert_ids, slot_index, saved_rows, row_rank, part_counts, w_gate, w_up, w_down):
    target = jnp.where(slot_index >= 0, expert_ids * CAP + slot_index, EXPERTS * CAP).astype(jnp.int32)
    target = target.reshape(EXPERTS, TOK_GRP)
    scaled = (gate_prob[:, None] * grad_out.astype(jnp.float32)).astype(jnp.bfloat16)
    scaled = scaled.reshape(EXPERTS, TOK_GRP, D)

    def bin_group(group_rows, where_to):
        padded_table = jnp.zeros((EXPERTS * CAP + 1, D), jnp.bfloat16).at[where_to].set(group_rows)
        return padded_table[:-1].reshape(EXPERTS, CAP, D)

    grad_bins = jnp.transpose(jax.vmap(bin_group)(scaled, target), (1, 0, 2, 3))

    def one_expert(operands):
        expert_bins, stored, positions, counts, gate_weight, up_weight, down_weight = operands
        slot_kept, row_index = locate(positions, counts)
        picked = jnp.take(stored, row_index.reshape(-1), axis=0)
        inputs = jnp.where(slot_kept.reshape(-1, 1), picked, 0).astype(jnp.bfloat16)
        partial_value, gate_wgrad, up_wgrad, down_wgrad = expert_grads(inputs, expert_bins.reshape(ROWS, D), gate_weight, up_weight, down_weight)
        return partial_value.astype(jnp.bfloat16).reshape(EXPERTS, CAP, D), gate_wgrad, up_wgrad, down_wgrad

    input_bins, grad_gate, grad_up, grad_down = lax.map(one_expert, (grad_bins, saved_rows, row_rank, part_counts, w_gate, w_up, w_down))
    returned = jnp.transpose(input_bins, (1, 0, 2, 3)).reshape(EXPERTS, EXPERTS * CAP, D)
    returned = jnp.concatenate([returned, jnp.zeros((EXPERTS, 1, D), jnp.bfloat16)], axis=1)
    grad_input = jax.vmap(lambda padded_table, where_to: jnp.take(padded_table, where_to, axis=0))(returned, target)
    return grad_input.reshape(TOKENS, D), grad_gate, grad_up, grad_down
```

```python
import functools

import jax
import jax.numpy as jnp
from jax import lax
from jax.experimental import pallas as pl
from jax.experimental.pallas import tpu as pltpu
from jax.sharding import PartitionSpec as P

MESH = pl.DeviceIdType.MESH
BF16, F32 = jnp.bfloat16, jnp.float32
OFFSETS = (-2, 3, -3, 4, -4, 5, -5, 6, -6, 7, -7, 8, 0, 1, -1, 2)


def kernel(
    cap,
    blocks,
    grad_ref,
    prob_ref,
    ids_ref,
    slot_ref,
    saved_ref,
    rank_ref,
    counts_ref,
    gate_hbm,
    up_hbm,
    down_hbm,
    dinput_hbm,
    dgate_hbm,
    dup_hbm,
    ddown_hbm,
    w_gate,
    w_up,
    w_down,
    token_hot,
    row_hot,
    bin_send,
    bin_recv,
    saved_recv,
    x_all,
    g_all,
    hidden_all,
    both_all,
    part_send,
    part_recv,
    half_send,
    half_recv,
    back_send,
    back_recv,
    dgate_out,
    dup_out,
    ddown_out,
    dinput_out,
    local_sem,
    send_sem,
    recv_sem,
):
    experts = lax.axis_size("expert")
    me, mx, my = lax.axis_index("expert"), lax.axis_index("dp"), lax.axis_index("tensor")
    ring = lax.axis_size("dp")
    keep = saved_ref.shape[1]
    slots = experts * cap
    rows = slots // blocks
    per_block = experts // blocks
    half = rows // 2
    wide = bin_send.shape[1]
    chunk = grad_ref.shape[1]
    tokens = grad_ref.shape[0]

    started = []
    counter = [0]

    def remote(src, dst, device):
        number = counter[0]
        counter[0] += 1
        copy = pltpu.make_async_remote_copy(
            src_ref=src,
            dst_ref=dst,
            send_sem=send_sem.at[number],
            recv_sem=recv_sem.at[number],
            device_id=device,
            device_id_type=MESH,
        )
        copy.start()
        started.append(copy)
        return copy

    def xdev(step):
        return {"dp": lax.rem(mx + ring + step, ring)}

    def ydev(step):
        return {"tensor": lax.rem(my + ring + step, ring)}

    def edev(step):
        return {"expert": lax.rem(me + experts + step, experts)}

    loads = [
        pltpu.make_async_copy(gate_hbm.at[0], w_gate, local_sem.at[0]),
        pltpu.make_async_copy(up_hbm.at[0], w_up, local_sem.at[1]),
        pltpu.make_async_copy(down_hbm.at[0], w_down, local_sem.at[2]),
    ]
    own_saved = pltpu.make_async_copy(
        saved_ref.at[0, :, pl.ds(pl.multiple_of((mx * ring + my) * chunk, chunk), chunk)],
        saved_recv.at[mx],
        local_sem.at[3],
    )
    own_saved.start()

    barrier = pltpu.get_barrier_semaphore()
    greeted = 0
    for step in range(1, ring):
        pl.semaphore_signal(barrier, inc=1, device_id=xdev(step), device_id_type=MESH)
        pl.semaphore_signal(barrier, inc=1, device_id=ydev(step), device_id_type=MESH)
        greeted += 2
    for step in range(1, experts):
        pl.semaphore_signal(barrier, inc=1, device_id=edev(step), device_id_type=MESH)
        greeted += 1
    for load in loads:
        load.start()

    ids, slot = ids_ref[...], slot_ref[...]
    target = jnp.where(slot >= 0, ids * wide + slot, -1)
    place = lax.broadcasted_iota(jnp.int32, (experts * wide, tokens), 0)
    token_hot[...] = jnp.where(place == target, 1.0, 0.0).astype(BF16)
    prob = jnp.broadcast_to(prob_ref[...], (chunk, tokens)).T
    scaled = (prob * grad_ref[...].astype(F32)).astype(BF16)
    bins = jnp.dot(token_hot[...], scaled, preferred_element_type=F32)
    bin_send[...] = bins.astype(BF16).reshape(experts, wide, chunk)

    pl.semaphore_wait(barrier, greeted)

    saved_copies = []
    for step in (2, 1, 3):
        to = lax.rem(mx + step, ring)
        columns = pl.ds(pl.multiple_of((to * ring + my) * chunk, chunk), chunk)
        saved_copies.append(
            remote(saved_ref.at[0, :, columns], saved_recv.at[mx], {"dp": to})
        )
    bin_copies = {}
    for spot, offset in enumerate(OFFSETS):
        if offset != 0:
            to = lax.rem(me + experts - offset, experts)
            bin_copies[spot] = remote(bin_send.at[to], bin_recv.at[spot], {"expert": to})

    lane = lax.broadcasted_iota(jnp.int32, (1, ring * keep), 1)
    position = jnp.full((1, ring * keep), -2, jnp.int32)
    before = jnp.int32(0)
    for part in range(ring):
        count = counts_ref[0, part]
        inside = (lane >= part * keep) & (lane < part * keep + count)
        position = jnp.where(inside, lane - part * keep + before, position)
        before = before + count
    position = position.astype(F32)
    diagonal = lax.broadcasted_iota(jnp.int32, (cap, cap), 0) == lax.broadcasted_iota(
        jnp.int32, (cap, cap), 1
    )
    for block in range(blocks):
        parts = []
        for spot in range(block * per_block, (block + 1) * per_block):
            group = lax.rem(me + experts + OFFSETS[spot], experts)
            rank = rank_ref[0, pl.ds(group, 1), :].astype(F32)
            column = jnp.sum(jnp.where(diagonal, rank, 0.0), axis=1, keepdims=True)
            parts.append(jnp.where(column == position, 1.0, 0.0))
        row_hot[pl.ds(block * rows, rows), :] = jnp.concatenate(parts, axis=0).astype(BF16)

    own_saved.wait()
    for copy in saved_copies:
        copy.wait_recv()

    x_first, g_first = {}, {}
    stored = saved_recv[...].reshape(ring * keep, chunk)
    for block in range(blocks):
        span = pl.ds(block * rows, rows)
        x_all[mx, my, span, :] = jnp.dot(
            row_hot[span, :], stored, preferred_element_type=F32
        ).astype(BF16)
        x_first[block] = [
            remote(x_all.at[mx, my, span], x_all.at[mx, my, span], xdev(step)) for step in (2, 1, 3)
        ]
    for block in range(blocks):
        span = pl.ds(block * rows, rows)
        parts = []
        for spot in range(block * per_block, (block + 1) * per_block):
            if OFFSETS[spot] == 0:
                piece = bin_send[me]
            else:
                bin_copies[spot].wait_recv()
                piece = bin_recv[spot]
            parts.append(piece.astype(F32)[:cap])
        g_all[mx, my, span, :] = jnp.concatenate(parts, axis=0).astype(BF16)
        g_first[block] = [
            remote(g_all.at[mx, my, span], g_all.at[mx, my, span], ydev(step)) for step in (2, 1, 3)
        ]

    near, far = {}, {}

    def spread(block):
        span = pl.ds(block * rows, rows)
        for copy in x_first[block]:
            copy.wait_recv()
        piece = x_all.at[:, my, span]
        x_near = [remote(piece, piece, ydev(1)), remote(piece, piece, ydev(-1))]
        for copy in g_first[block]:
            copy.wait_recv()
        piece = g_all.at[mx, :, span]
        g_near = [remote(piece, piece, xdev(1)), remote(piece, piece, xdev(-1))]
        near[block] = (x_near, g_near)

    def forward(block):
        span = pl.ds(block * rows, rows)
        low, high = lax.rem(my + ring - 1, ring), lax.rem(my + 1, ring)
        x_near, g_near = near[block]
        x_near[0].wait_recv()
        piece = x_all.at[pl.ds(0, ring // 2), low, span]
        copies = [remote(piece, piece, ydev(1))]
        x_near[1].wait_recv()
        piece = x_all.at[pl.ds(ring // 2, ring // 2), high, span]
        copies.append(remote(piece, piece, ydev(-1)))
        low, high = lax.rem(mx + ring - 1, ring), lax.rem(mx + 1, ring)
        g_near[0].wait_recv()
        piece = g_all.at[low, pl.ds(0, ring // 2), span]
        copies.append(remote(piece, piece, xdev(1)))
        g_near[1].wait_recv()
        piece = g_all.at[high, pl.ds(ring // 2, ring // 2), span]
        copies.append(remote(piece, piece, xdev(-1)))
        far[block] = copies

    part_copies, half_copies, back_copies = {}, {}, {}

    def compute(block):
        span = pl.ds(block * rows, rows)
        for copy in far[block]:
            copy.wait_recv()
        inputs = jnp.concatenate(
            [x_all[c // ring, c % ring, span, :] for c in range(ring * ring)], axis=1
        )
        gate_pre = jnp.dot(inputs, w_gate[...], preferred_element_type=F32)
        up_pre = jnp.dot(inputs, w_up[...], preferred_element_type=F32)
        grads = jnp.concatenate(
            [g_all[c // ring, c % ring, span, :] for c in range(ring * ring)], axis=1
        )
        hidden_grad = lax.dot_general(
            grads, w_down[...], (((1,), (1,)), ((), ())), preferred_element_type=F32
        )
        squash = 1.0 / (1.0 + jnp.exp(-gate_pre))
        activated = gate_pre * squash
        hidden_all[span, :] = (activated * up_pre).astype(BF16)
        up_grad = (hidden_grad * activated).astype(BF16)
        gate_grad = (hidden_grad * up_pre * squash * (1.0 + gate_pre * (1.0 - squash))).astype(BF16)
        units = gate_grad.shape[1]
        both_all[span, pl.ds(0, units)] = gate_grad
        both_all[span, pl.ds(units, units)] = up_grad
        for x in range(ring):
            piece = pl.ds(x * ring * chunk, ring * chunk)
            total = lax.dot_general(
                gate_grad, w_gate[piece, :], (((1,), (1,)), ((), ())), preferred_element_type=F32
            ) + lax.dot_general(
                up_grad, w_up[piece, :], (((1,), (1,)), ((), ())), preferred_element_type=F32
            )
            total = total.astype(BF16)
            for y in range(ring):
                part_send[block, x, y] = total[:, y * chunk : (y + 1) * chunk]
        first, second = pl.ds(0, half), pl.ds(half, half)
        copies = []
        for step in (2, 1, 3):
            to = lax.rem(mx + step, ring)
            copies.append(
                remote(
                    part_send.at[block, to, :, first],
                    part_recv.at[block, 0, step - 1],
                    {"dp": to},
                )
            )
            to = lax.rem(my + step, ring)
            copies.append(
                remote(
                    part_send.at[block, :, to, second],
                    part_recv.at[block, 1, step - 1],
                    {"tensor": to},
                )
            )
        part_copies[block] = copies

    def reduce_first(block):
        first, second = pl.ds(0, half), pl.ds(half, half)
        copies = part_copies[block]
        for copy in copies[0::2]:
            copy.wait_recv()
        total = part_send[block, mx, :, first, :].astype(F32)
        for step in range(ring - 1):
            total = total + part_recv[block, 0, step].astype(F32)
        half_send[block, 0] = total.astype(BF16)
        sent = []
        for step in (2, 1, 3):
            to = lax.rem(my + step, ring)
            sent.append(
                remote(half_send.at[block, 0, to], half_recv.at[block, 0, step - 1], {"tensor": to})
            )
        for copy in copies[1::2]:
            copy.wait_recv()
        total = part_send[block, :, my, second, :].astype(F32)
        for step in range(ring - 1):
            total = total + part_recv[block, 1, step].astype(F32)
        half_send[block, 1] = total.astype(BF16)
        for step in (2, 1, 3):
            to = lax.rem(mx + step, ring)
            sent.append(
                remote(half_send.at[block, 1, to], half_recv.at[block, 1, step - 1], {"dp": to})
            )
        half_copies[block] = sent

    def reduce_second(block):
        spare = jnp.zeros((wide - cap, chunk), F32)
        for which, own in ((0, my), (1, mx)):
            for copy in half_copies[block][3 * which : 3 * which + 3]:
                copy.wait_recv()
            total = half_send[block, which, own].astype(F32)
            for step in range(ring - 1):
                total = total + half_recv[block, which, step].astype(F32)
            for inner in range(per_block // 2):
                spot = block * per_block + which * (per_block // 2) + inner
                piece = jnp.concatenate([total[inner * cap : (inner + 1) * cap], spare], axis=0)
                if OFFSETS[spot] == 0:
                    back_recv[me] = piece.astype(BF16)
                else:
                    back_send[spot] = piece.astype(BF16)
                    to = lax.rem(me + experts + OFFSETS[spot], experts)
                    back_copies[spot] = remote(
                        back_send.at[spot], back_recv.at[me], {"expert": to}
                    )

    outs = []

    def store(src, dst, number):
        copy = pltpu.make_async_copy(src, dst, local_sem.at[number])
        copy.start()
        outs.append(copy)

    def weight_grads_in():
        units = w_gate.shape[1]
        for c in range(ring * ring):
            both = lax.dot_general(
                x_all[c // ring, c % ring],
                both_all[...],
                (((0,), (0,)), ((), ())),
                preferred_element_type=F32,
            ).astype(BF16)
            dgate_out[pl.ds(c * chunk, chunk), :] = both[:, :units]
            dup_out[pl.ds(c * chunk, chunk), :] = both[:, units:]
        store(dgate_out, dgate_hbm.at[0], 4)
        store(dup_out, dup_hbm.at[0], 5)

    def weight_grads_out():
        hidden = hidden_all[...].astype(F32).T.astype(BF16)
        for c in range(0, ring * ring, 2):
            pair = jnp.concatenate(
                [g_all[c // ring, c % ring], g_all[(c + 1) // ring, (c + 1) % ring]], axis=1
            )
            ddown_out[:, pl.ds(c * chunk, 2 * chunk)] = jnp.dot(
                hidden, pair, preferred_element_type=F32
            ).astype(BF16)
        store(ddown_out, ddown_hbm.at[0], 6)

    for load in loads:
        load.wait()
    spread(0)
    for block in range(blocks + 3):
        if block + 1 < blocks:
            spread(block + 1)
        if block < blocks:
            forward(block)
        if 0 <= block - 1 < blocks:
            compute(block - 1)
        if 0 <= block - 2 < blocks:
            if block - 2 == blocks - 1:
                weight_grads_in()
            reduce_first(block - 2)
        if 0 <= block - 3 < blocks:
            if block - 3 == blocks - 1:
                weight_grads_out()
            reduce_second(block - 3)

    for copy in back_copies.values():
        copy.wait_recv()
    returned = back_recv[...].reshape(experts * wide, chunk)
    dinput_out[...] = lax.dot_general(
        token_hot[...], returned, (((0,), (0,)), ((), ())), preferred_element_type=F32
    ).astype(BF16)
    store(dinput_out, dinput_hbm, 7)
    for copy in started:
        copy.wait_send()
    for copy in outs:
        copy.wait()


def local(
    grad_out,
    gate_prob,
    expert_ids,
    slot_index,
    saved_rows,
    row_rank,
    part_counts,
    w_gate,
    w_up,
    w_down,
):
    experts, cap = row_rank.shape[1], row_rank.shape[2]
    tokens, chunk = grad_out.shape
    ring = part_counts.shape[1]
    keep = saved_rows.shape[1]
    width, units = w_gate.shape[1], w_gate.shape[2]
    blocks = 4
    slots = experts * cap
    rows = slots // blocks
    wide = 48
    copies = 2 * (experts - 1) + 3 + blocks * (6 + 8 + 12)
    vmem = pl.BlockSpec(memory_space=pltpu.VMEM)
    anywhere = pl.BlockSpec(memory_space=pl.ANY)
    return pl.pallas_call(
        functools.partial(kernel, cap, blocks),
        out_shape=(
            jax.ShapeDtypeStruct((tokens, chunk), BF16),
            jax.ShapeDtypeStruct(w_gate.shape, BF16),
            jax.ShapeDtypeStruct(w_up.shape, BF16),
            jax.ShapeDtypeStruct(w_down.shape, BF16),
        ),
        in_specs=[
            vmem,
            vmem,
            vmem,
            vmem,
            anywhere,
            vmem,
            pl.BlockSpec(memory_space=pltpu.SMEM),
            anywhere,
            anywhere,
            anywhere,
        ],
        out_specs=(anywhere,) * 4,
        scratch_shapes=[
            pltpu.VMEM((width, units), BF16),
            pltpu.VMEM((width, units), BF16),
            pltpu.VMEM((units, width), BF16),
            pltpu.VMEM((experts * wide, tokens), BF16),
            pltpu.VMEM((slots, ring * keep), BF16),
            pltpu.VMEM((experts, wide, chunk), BF16),
            pltpu.VMEM((experts, wide, chunk), BF16),
            pltpu.VMEM((ring, keep, chunk), BF16),
            pltpu.VMEM((ring, ring, slots, chunk), BF16),
            pltpu.VMEM((ring, ring, slots, chunk), BF16),
            pltpu.VMEM((slots, units), BF16),
            pltpu.VMEM((slots, 2 * units), BF16),
            pltpu.VMEM((blocks, ring, ring, rows, chunk), BF16),
            pltpu.VMEM((blocks, 2, ring - 1, ring, rows // 2, chunk), BF16),
            pltpu.VMEM((blocks, 2, ring, rows // 2, chunk), BF16),
            pltpu.VMEM((blocks, 2, ring - 1, rows // 2, chunk), BF16),
            pltpu.VMEM((experts, wide, chunk), BF16),
            pltpu.VMEM((experts, wide, chunk), BF16),
            pltpu.VMEM((width, units), BF16),
            pltpu.VMEM((width, units), BF16),
            pltpu.VMEM((units, width), BF16),
            pltpu.VMEM((tokens, chunk), BF16),
            pltpu.SemaphoreType.DMA((8,)),
            pltpu.SemaphoreType.DMA((copies,)),
            pltpu.SemaphoreType.DMA((copies,)),
        ],
        compiler_params=pltpu.CompilerParams(
            collective_id=0, has_side_effects=True, vmem_limit_bytes=56 << 20
        ),
        name="experts_backward",
    )(
        grad_out,
        gate_prob.reshape(1, tokens),
        expert_ids.reshape(1, tokens),
        slot_index.reshape(1, tokens),
        saved_rows,
        row_rank,
        part_counts,
        w_gate,
        w_up,
        w_down,
    )


def solution(mesh):
    placed = (
        P("expert", ("dp", "tensor")),
        P("expert"),
        P("expert"),
        P("expert"),
        P("expert", "dp", None),
        P("expert", None, None),
        P("expert", None),
        P("expert", None, ("dp", "tensor")),
        P("expert", None, ("dp", "tensor")),
        P("expert", ("dp", "tensor"), None),
    )
    return jax.shard_map(
        local,
        mesh=mesh,
        in_specs=placed,
        out_specs=(
            P("expert", ("dp", "tensor")),
            P("expert", None, ("dp", "tensor")),
            P("expert", None, ("dp", "tensor")),
            P("expert", ("dp", "tensor"), None),
        ),
        check_vma=False,
    )
```

```python
import functools

import jax
import jax.numpy as jnp
from jax import lax
from jax.experimental import pallas as pl
from jax.experimental.pallas import tpu as pltpu
from jax.sharding import PartitionSpec as P

MESH = pl.DeviceIdType.MESH
BF16, F32 = jnp.bfloat16, jnp.float32
BLOCKS = (4, 4, 4, 4)
DIRECT_SHARES = 1
DIRECT_SUMS = 1
OFFSETS = (-2, 3, -3, 4, -4, 5, -5, 6, -6, 7, -7, 8, 0, 1, -1, 2)


def kernel(
    cap,
    grad_hbm,
    prob_hbm,
    ids_hbm,
    slot_hbm,
    saved_ref,
    rank_hbm,
    counts_hbm,
    gate_hbm,
    up_hbm,
    down_hbm,
    dinput_out,
    dgate_out,
    dup_out,
    ddown_out,
    grad_ref,
    prob_ref,
    ids_ref,
    slot_ref,
    rank_ref,
    counts_ref,
    w_gate,
    w_up,
    w_down,
    token_hot,
    row_hot,
    bin_send,
    bin_recv,
    saved_recv,
    x_all,
    g_all,
    hidden_all,
    both_all,
    part_send,
    fold_recv,
    part_recv,
    half_send,
    half_recv,
    back_send,
    back_recv,
    local_sem,
    send_sem,
    recv_sem,
):
    experts = lax.axis_size("expert")
    me, mx, my = lax.axis_index("expert"), lax.axis_index("dp"), lax.axis_index("tensor")
    ring = lax.axis_size("dp")
    keep = saved_ref.shape[1]
    wide = bin_send.shape[1]
    tokens, chunk = grad_ref.shape
    units = w_gate.shape[1]
    last = len(BLOCKS) - 1
    first_group = [sum(BLOCKS[:block]) for block in range(len(BLOCKS))]

    def rows_of(block):
        return first_group[block] * cap, BLOCKS[block] * cap

    def span_of(block):
        return pl.ds(*rows_of(block))

    def halves_of(block):
        start, size = rows_of(block)
        cut = size // 32 * 16
        return (pl.ds(start, cut), pl.ds(start + cut, size - cut))

    started = []

    def remote(src, dst, device):
        number = len(started)
        copy = pltpu.make_async_remote_copy(
            src_ref=src,
            dst_ref=dst,
            send_sem=send_sem.at[number],
            recv_sem=recv_sem.at[number],
            device_id=device,
            device_id_type=MESH,
        )
        copy.start()
        started.append(copy)
        return copy

    def xdev(step):
        return {"dp": lax.rem(mx + ring + step, ring)}

    def ydev(step):
        return {"tensor": lax.rem(my + ring + step, ring)}

    def edev(step):
        return {"expert": lax.rem(me + experts + step, experts)}

    small = [
        pltpu.make_async_copy(src, dst, local_sem.at[number])
        for number, (src, dst) in enumerate(
            (
                (grad_hbm, grad_ref),
                (prob_hbm, prob_ref),
                (ids_hbm, ids_ref),
                (slot_hbm, slot_ref),
                (rank_hbm.at[0], rank_ref),
                (counts_hbm, counts_ref),
                (
                    saved_ref.at[0, :, pl.ds(pl.multiple_of((mx * ring + my) * chunk, chunk), chunk)],
                    saved_recv.at[mx],
                ),
            )
        )
    ]
    loads = [
        pltpu.make_async_copy(src.at[0], dst, local_sem.at[len(small) + number])
        for number, (src, dst) in enumerate(((gate_hbm, w_gate), (up_hbm, w_up), (down_hbm, w_down)))
    ]
    for load in small:
        load.start()

    barrier = pltpu.get_barrier_semaphore()
    greeted = 0
    for step in range(1, ring):
        pl.semaphore_signal(barrier, inc=1, device_id=xdev(step), device_id_type=MESH)
        pl.semaphore_signal(barrier, inc=1, device_id=ydev(step), device_id_type=MESH)
        greeted += 2
    for step in range(1, experts):
        pl.semaphore_signal(barrier, inc=1, device_id=edev(step), device_id_type=MESH)
        greeted += 1
    for load in loads:
        load.start()
    for load in small:
        load.wait()

    ids, slot = ids_ref[...], slot_ref[...]
    target = jnp.where(slot >= 0, ids * wide + slot, -1)
    place = lax.broadcasted_iota(jnp.int32, (experts * wide, tokens), 0)
    token_hot[...] = jnp.where(place == target, 1.0, 0.0).astype(BF16)
    prob = jnp.broadcast_to(prob_ref[...], (chunk, tokens)).T
    scaled = (prob * grad_ref[...].astype(F32)).astype(BF16)
    bins = jnp.dot(token_hot[...], scaled, preferred_element_type=F32)
    bin_send[...] = bins.astype(BF16).reshape(experts, wide, chunk)

    pl.semaphore_wait(barrier, greeted)

    saved_copies = []
    for step in (2, 1, 3):
        to = lax.rem(mx + step, ring)
        columns = pl.ds(pl.multiple_of((to * ring + my) * chunk, chunk), chunk)
        saved_copies.append(
            remote(saved_ref.at[0, :, columns], saved_recv.at[mx], {"dp": to})
        )
    bin_copies = {}
    for spot, offset in enumerate(OFFSETS):
        if offset != 0:
            to = lax.rem(me + experts - offset, experts)
            bin_copies[spot] = remote(bin_send.at[to], bin_recv.at[spot], {"expert": to})

    lane = lax.broadcasted_iota(jnp.int32, (1, ring * keep), 1)
    position = jnp.full((1, ring * keep), -2, jnp.int32)
    before = jnp.zeros((1, 1), jnp.int32)
    for part in range(ring):
        count = counts_ref[:, part : part + 1]
        inside = (lane >= part * keep) & (lane < part * keep + count)
        position = jnp.where(inside, lane - part * keep + before, position)
        before = before + count
    position = position.astype(F32)
    diagonal = lax.broadcasted_iota(jnp.int32, (cap, cap), 0) == lax.broadcasted_iota(
        jnp.int32, (cap, cap), 1
    )
    for block in range(len(BLOCKS)):
        parts = []
        for spot in range(first_group[block], first_group[block] + BLOCKS[block]):
            group = lax.rem(me + experts + OFFSETS[spot], experts)
            rank = rank_ref[pl.ds(group, 1), :].astype(F32)
            column = jnp.sum(jnp.where(diagonal, rank, 0.0), axis=1, keepdims=True)
            parts.append(jnp.where(column == position, 1.0, 0.0))
        row_hot[span_of(block), :] = jnp.concatenate(parts, axis=0).astype(BF16)

    x_first, g_first = {}, {}

    def share(block, ref, device):
        piece = ref.at[mx, my, span_of(block)]
        return [remote(piece, piece, device(step)) for step in ((2, 1, 3) if block < DIRECT_SHARES else (1, 3))]

    def pick_x(block):
        if block == 0:
            for copy in saved_copies:
                copy.wait_recv()
        span = span_of(block)
        x_all[mx, my, span, :] = jnp.dot(
            row_hot[span, :], saved_recv[...].reshape(ring * keep, chunk), preferred_element_type=F32
        ).astype(BF16)
        x_first[block] = share(block, x_all, xdev)

    def pick_g(block):
        parts = []
        for spot in range(first_group[block], first_group[block] + BLOCKS[block]):
            if OFFSETS[spot] == 0:
                piece = bin_send[me]
            else:
                bin_copies[spot].wait_recv()
                piece = bin_recv[spot]
            parts.append(piece.astype(F32)[:cap])
        g_all[mx, my, span_of(block), :] = jnp.concatenate(parts, axis=0).astype(BF16)
        g_first[block] = share(block, g_all, ydev)

    low_x, high_x = lax.rem(mx + ring - 1, ring), lax.rem(mx + 1, ring)
    low_y, high_y = lax.rem(my + ring - 1, ring), lax.rem(my + 1, ring)

    def relay(block):
        if block < DIRECT_SHARES:
            return
        first, second = halves_of(block)
        for copies, ref, low, high, device in (
            (x_first, x_all, (low_x, my), (high_x, my), xdev),
            (g_first, g_all, (mx, low_y), (mx, high_y), ydev),
        ):
            up, down = copies[block]
            up.wait_recv()
            piece = ref.at[low[0], low[1], first]
            sent = [remote(piece, piece, device(1))]
            down.wait_recv()
            piece = ref.at[high[0], high[1], second]
            sent.append(remote(piece, piece, device(-1)))
            copies[block] = sent

    near, far = {}, {}

    def spread(block):
        span = span_of(block)
        for copy in x_first[block]:
            copy.wait_recv()
        piece = x_all.at[:, my, span]
        x_near = [remote(piece, piece, ydev(1)), remote(piece, piece, ydev(-1))]
        for copy in g_first[block]:
            copy.wait_recv()
        piece = g_all.at[mx, :, span]
        g_near = [remote(piece, piece, xdev(1)), remote(piece, piece, xdev(-1))]
        near[block] = (x_near, g_near)

    low_half, high_half = pl.ds(0, ring // 2), pl.ds(ring // 2, ring // 2)

    def forward(block):
        span = span_of(block)
        x_near, g_near = near[block]
        x_near[0].wait_recv()
        piece = x_all.at[low_half, low_y, span]
        copies = [remote(piece, piece, ydev(1))]
        x_near[1].wait_recv()
        piece = x_all.at[high_half, high_y, span]
        copies.append(remote(piece, piece, ydev(-1)))
        g_near[0].wait_recv()
        piece = g_all.at[low_x, low_half, span]
        copies.append(remote(piece, piece, xdev(1)))
        g_near[1].wait_recv()
        piece = g_all.at[high_x, high_half, span]
        copies.append(remote(piece, piece, xdev(-1)))
        far[block] = copies

    def along(which, index, others, span):
        return part_send.at[(index, others, span) if which == 0 else (others, index, span)]

    lines = (
        (xdev, mx, low_x, high_x, ydev, my),
        (ydev, my, low_y, high_y, xdev, mx),
    )
    part_copies, half_copies, back_copies = {}, {}, {}

    def compute(block):
        span = span_of(block)
        for copy in far[block]:
            copy.wait_recv()
        inputs = jnp.concatenate(
            [x_all[c // ring, c % ring, span, :] for c in range(ring * ring)], axis=1
        )
        gate_pre = jnp.dot(inputs, w_gate[...], preferred_element_type=F32)
        up_pre = jnp.dot(inputs, w_up[...], preferred_element_type=F32)
        grads = jnp.concatenate(
            [g_all[c // ring, c % ring, span, :] for c in range(ring * ring)], axis=1
        )
        hidden_grad = lax.dot_general(
            grads, w_down[...], (((1,), (1,)), ((), ())), preferred_element_type=F32
        )
        squash = 1.0 / (1.0 + jnp.exp(-gate_pre))
        activated = gate_pre * squash
        hidden_all[span, :] = (activated * up_pre).astype(BF16)
        up_grad = (hidden_grad * activated).astype(BF16)
        gate_grad = (hidden_grad * up_pre * squash * (1.0 + gate_pre * (1.0 - squash))).astype(BF16)
        both_all[span, pl.ds(0, units)] = gate_grad
        both_all[span, pl.ds(units, units)] = up_grad
        for x in range(ring):
            piece = pl.ds(x * ring * chunk, ring * chunk)
            total = lax.dot_general(
                gate_grad, w_gate[piece, :], (((1,), (1,)), ((), ())), preferred_element_type=F32
            ) + lax.dot_general(
                up_grad, w_up[piece, :], (((1,), (1,)), ((), ())), preferred_element_type=F32
            )
            total = total.astype(BF16)
            for y in range(ring):
                part_send[x, y, span, :] = total[:, y * chunk : (y + 1) * chunk]
        copies = [[], []]
        for which, span in enumerate(halves_of(block)):
            device, mine, low, high = lines[which][:4]
            if block > last - DIRECT_SUMS:
                for step in (2, 1, 3):
                    to = lax.rem(mine + step, ring)
                    copies[which].append(
                        remote(
                            along(which, to, slice(None), span),
                            part_recv.at[step - 1, :, span],
                            device(step),
                        )
                    )
                continue
            other = lax.rem(mine + 2, ring)
            copies[which] = [
                remote(along(which, other, low_half, span), fold_recv.at[0, :, span], device(1)),
                remote(along(which, other, high_half, span), fold_recv.at[1, :, span], device(-1)),
                remote(
                    along(which, high, high_half, span), part_recv.at[0, high_half, span], device(1)
                ),
                remote(
                    along(which, low, low_half, span), part_recv.at[1, low_half, span], device(-1)
                ),
            ]
        part_copies[block] = copies

    def fold(block):
        if block > last - DIRECT_SUMS:
            return
        for which, span in enumerate(halves_of(block)):
            device, mine, low, high = lines[which][:4]
            copies = part_copies[block][which]
            for number, (index, others, step) in enumerate(
                ((high, low_half, 1), (low, high_half, -1))
            ):
                copies[number].wait_recv()
                piece = along(which, index, others, span)
                piece[...] = (
                    piece[...].astype(F32) + fold_recv[number, :, span, :].astype(F32)
                ).astype(BF16)
                copies.append(remote(piece, part_recv.at[number, others, span], device(step)))
            part_copies[block][which] = copies[2:]

    def reduce_first(block):
        sent = [[], []]
        for which, span in enumerate(halves_of(block)):
            mine = lines[which][1]
            device, own = lines[which][4:]
            for copy in part_copies[block][which]:
                copy.wait_recv()
            total = along(which, mine, slice(None), span)[...].astype(F32)
            for step in range(ring - 1 if block > last - DIRECT_SUMS else 2):
                total = total + part_recv[step, :, span, :].astype(F32)
            half_send[:, span, :] = total.astype(BF16)
            for step in (2, 1, 3):
                to = lax.rem(own + step, ring)
                sent[which].append(
                    remote(half_send.at[to, span], half_recv.at[step - 1, span], device(step))
                )
        half_copies[block] = sent

    def reduce_second(block):
        spare = jnp.zeros((wide - cap, chunk), F32)
        totals = []
        for which, span in enumerate(halves_of(block)):
            own = lines[which][5]
            for copy in half_copies[block][which]:
                copy.wait_recv()
            total = half_send[own, span, :].astype(F32)
            for step in range(ring - 1):
                total = total + half_recv[step, span, :].astype(F32)
            totals.append(total)
        total = jnp.concatenate(totals, axis=0)
        for inner in range(BLOCKS[block]):
            spot = first_group[block] + inner
            piece = jnp.concatenate([total[inner * cap : (inner + 1) * cap], spare], axis=0)
            if OFFSETS[spot] == 0:
                back_recv[me] = piece.astype(BF16)
            else:
                back_send[spot] = piece.astype(BF16)
                back_copies[spot] = remote(
                    back_send.at[spot], back_recv.at[me], edev(OFFSETS[spot])
                )

    def weight_grads_in():
        for c in range(ring * ring):
            both = lax.dot_general(
                x_all[c // ring, c % ring],
                both_all[...],
                (((0,), (0,)), ((), ())),
                preferred_element_type=F32,
            ).astype(BF16)
            dgate_out[0, pl.ds(c * chunk, chunk), :] = both[:, :units]
            dup_out[0, pl.ds(c * chunk, chunk), :] = both[:, units:]

    def weight_grads_out():
        hidden = hidden_all[...].astype(F32).T.astype(BF16)
        for c in range(0, ring * ring, 2):
            pair = jnp.concatenate(
                [g_all[c // ring, c % ring], g_all[(c + 1) // ring, (c + 1) % ring]], axis=1
            )
            ddown_out[0, :, pl.ds(c * chunk, 2 * chunk)] = jnp.dot(
                hidden, pair, preferred_element_type=F32
            ).astype(BF16)

    count = len(BLOCKS)
    pick_g(0)
    pick_g(1)
    pick_x(0)
    pick_x(1)
    for block in range(2, count):
        pick_g(block)
        pick_x(block)
    for load in loads:
        load.wait()
    stages = ((relay, -2), (spread, -1), (forward, 0), (compute, 1), (fold, 2), (reduce_first, 3), (reduce_second, 4))
    for turn in range(-2, count + 3):
        if turn == count + 1:
            weight_grads_in()
        if turn == count + 2:
            weight_grads_out()
        for stage, lag in stages:
            block = turn - lag
            if stage in (reduce_first, reduce_second):
                if 0 <= block < last:
                    stage(block)
                if block + 1 == last:
                    stage(last)
            elif 0 <= block < count:
                stage(block)

    for copy in back_copies.values():
        copy.wait_recv()
    returned = back_recv[...].reshape(experts * wide, chunk)
    dinput_out[...] = lax.dot_general(
        token_hot[...], returned, (((0,), (0,)), ((), ())), preferred_element_type=F32
    ).astype(BF16)
    for copy in started:
        copy.wait_send()


def write_out(*refs):
    sources, targets, sem = refs[:4], refs[4:8], refs[8]
    copies = []
    for source, target in zip(sources, targets):
        if len(source.shape) == 2:
            copies.append((source, target))
        else:
            size = source.shape[1] // 4
            for part in range(4):
                piece = pl.ds(part * size, size)
                copies.append((source.at[:, piece], target.at[:, piece]))
    copies = [
        pltpu.make_async_copy(source, target, sem.at[number])
        for number, (source, target) in enumerate(copies)
    ]
    for copy in copies:
        copy.start()
    for copy in copies:
        copy.wait()


def local(
    grad_out,
    gate_prob,
    expert_ids,
    slot_index,
    saved_rows,
    row_rank,
    part_counts,
    w_gate,
    w_up,
    w_down,
):
    experts, cap = row_rank.shape[1], row_rank.shape[2]
    tokens, chunk = grad_out.shape
    ring = part_counts.shape[1]
    keep = saved_rows.shape[1]
    width, units = w_gate.shape[1], w_gate.shape[2]
    slots = experts * cap
    wide = 48
    copies = 2 * (experts - 1) + 3 + len(BLOCKS) * (8 + 8 + 12 + 6)
    vmem = pl.BlockSpec(memory_space=pltpu.VMEM)
    anywhere = pl.BlockSpec(memory_space=pl.ANY)
    held = pl.pallas_call(
        functools.partial(kernel, cap),
        out_shape=(
            pltpu.VMEM((tokens, chunk), BF16),
            pltpu.VMEM(w_gate.shape, BF16),
            pltpu.VMEM(w_up.shape, BF16),
            pltpu.VMEM(w_down.shape, BF16),
        ),
        in_specs=[anywhere] * 10,
        out_specs=(vmem,) * 4,
        scratch_shapes=[
            pltpu.VMEM((tokens, chunk), BF16),
            pltpu.VMEM((1, tokens), F32),
            pltpu.VMEM((1, tokens), jnp.int32),
            pltpu.VMEM((1, tokens), jnp.int32),
            pltpu.VMEM((experts, cap), jnp.int32),
            pltpu.VMEM((1, ring), jnp.int32),
            pltpu.VMEM((width, units), BF16),
            pltpu.VMEM((width, units), BF16),
            pltpu.VMEM((units, width), BF16),
            pltpu.VMEM((experts * wide, tokens), BF16),
            pltpu.VMEM((slots, ring * keep), BF16),
            pltpu.VMEM((experts, wide, chunk), BF16),
            pltpu.VMEM((experts, wide, chunk), BF16),
            pltpu.VMEM((ring, keep, chunk), BF16),
            pltpu.VMEM((ring, ring, slots, chunk), BF16),
            pltpu.VMEM((ring, ring, slots, chunk), BF16),
            pltpu.VMEM((slots, units), BF16),
            pltpu.VMEM((slots, 2 * units), BF16),
            pltpu.VMEM((ring, ring, slots, chunk), BF16),
            pltpu.VMEM((2, ring // 2, slots, chunk), BF16),
            pltpu.VMEM((ring - 1, ring, slots, chunk), BF16),
            pltpu.VMEM((ring, slots, chunk), BF16),
            pltpu.VMEM((ring - 1, slots, chunk), BF16),
            pltpu.VMEM((experts, wide, chunk), BF16),
            pltpu.VMEM((experts, wide, chunk), BF16),
            pltpu.SemaphoreType.DMA((10,)),
            pltpu.SemaphoreType.DMA((copies,)),
            pltpu.SemaphoreType.DMA((copies,)),
        ],
        compiler_params=pltpu.CompilerParams(
            collective_id=0, has_side_effects=True, vmem_limit_bytes=52 << 20
        ),
        name="experts_backward",
    )(
        grad_out,
        gate_prob.reshape(1, tokens),
        expert_ids.reshape(1, tokens),
        slot_index.reshape(1, tokens),
        saved_rows,
        row_rank,
        part_counts,
        w_gate,
        w_up,
        w_down,
    )
    held = [pltpu.with_memory_space_constraint(part, pltpu.VMEM) for part in held]
    return pl.pallas_call(
        write_out,
        out_shape=tuple(jax.ShapeDtypeStruct(part.shape, part.dtype) for part in held),
        in_specs=[vmem] * 4,
        out_specs=(anywhere,) * 4,
        scratch_shapes=[pltpu.SemaphoreType.DMA((13,))],
        name="write_out",
    )(*held)


def solution(mesh):
    placed = (
        P("expert", ("dp", "tensor")),
        P("expert"),
        P("expert"),
        P("expert"),
        P("expert", "dp", None),
        P("expert", None, None),
        P("expert", None),
        P("expert", None, ("dp", "tensor")),
        P("expert", None, ("dp", "tensor")),
        P("expert", ("dp", "tensor"), None),
    )
    return jax.shard_map(
        local,
        mesh=mesh,
        in_specs=placed,
        out_specs=(
            P("expert", ("dp", "tensor")),
            P("expert", None, ("dp", "tensor")),
            P("expert", None, ("dp", "tensor")),
            P("expert", ("dp", "tensor"), None),
        ),
        check_vma=False,
    )
```

```python
import functools

import jax
import jax.numpy as jnp
from jax import lax
from jax.experimental import pallas as pl
from jax.experimental.pallas import tpu as pltpu
from jax.sharding import PartitionSpec as P

MESH = pl.DeviceIdType.MESH
BF16, F32 = jnp.bfloat16, jnp.float32
BLOCKS = (4, 4, 4, 4)
DIRECT_SHARES = 1
DIRECT_SUMS = 1
SPLIT = 2.5
OFFSETS = (-2, 3, -3, 4, -4, 5, -5, 6, -6, 7, -7, 8, 0, 1, -1, 2)


def kernel(
    cap,
    grad_hbm,
    prob_hbm,
    ids_hbm,
    slot_hbm,
    saved_ref,
    rank_hbm,
    counts_hbm,
    gate_hbm,
    up_hbm,
    down_hbm,
    dinput_out,
    dgate_out,
    dup_out,
    ddown_out,
    grad_ref,
    prob_ref,
    ids_ref,
    slot_ref,
    rank_ref,
    counts_ref,
    w_gate,
    w_up,
    w_down,
    token_hot,
    token_hot_t,
    w_down_t,
    w_both_t,
    row_hot,
    bin_send,
    bin_recv,
    saved_recv,
    x_all,
    g_all,
    hidden_all,
    both_all,
    part_send,
    fold_recv,
    part_recv,
    half_send,
    half_recv,
    back_send,
    back_recv,
    local_sem,
    send_sem,
    recv_sem,
):
    experts = lax.axis_size("expert")
    me, mx, my = lax.axis_index("expert"), lax.axis_index("dp"), lax.axis_index("tensor")
    ring = lax.axis_size("dp")
    keep = saved_ref.shape[1]
    wide = bin_send.shape[1]
    tokens, chunk = grad_ref.shape
    units = w_gate.shape[1]
    last = len(BLOCKS) - 1
    first_group = [sum(BLOCKS[:block]) for block in range(len(BLOCKS))]

    def rows_of(block):
        return first_group[block] * cap, BLOCKS[block] * cap

    def span_of(block):
        return pl.ds(*rows_of(block))

    def halves_of(block, share=2.5):
        start, size = rows_of(block)
        cut = int(size * share / 5) // 16 * 16
        return (pl.ds(start, cut), pl.ds(start + cut, size - cut))

    started = []

    def remote(src, dst, device):
        number = len(started)
        copy = pltpu.make_async_remote_copy(
            src_ref=src,
            dst_ref=dst,
            send_sem=send_sem.at[number],
            recv_sem=recv_sem.at[number],
            device_id=device,
            device_id_type=MESH,
        )
        copy.start()
        started.append(copy)
        return copy

    def xdev(step):
        return {"dp": lax.rem(mx + ring + step, ring)}

    def ydev(step):
        return {"tensor": lax.rem(my + ring + step, ring)}

    def edev(step):
        return {"expert": lax.rem(me + experts + step, experts)}

    small = [
        pltpu.make_async_copy(src, dst, local_sem.at[number])
        for number, (src, dst) in enumerate(
            (
                (grad_hbm, grad_ref),
                (prob_hbm, prob_ref),
                (ids_hbm, ids_ref),
                (slot_hbm, slot_ref),
                (rank_hbm.at[0], rank_ref),
                (counts_hbm, counts_ref),
                (
                    saved_ref.at[0, :, pl.ds(pl.multiple_of((mx * ring + my) * chunk, chunk), chunk)],
                    saved_recv.at[mx],
                ),
            )
        )
    ]
    loads = [
        pltpu.make_async_copy(src.at[0], dst, local_sem.at[len(small) + number])
        for number, (src, dst) in enumerate(((gate_hbm, w_gate), (up_hbm, w_up), (down_hbm, w_down)))
    ]
    for load in small:
        load.start()

    barrier = pltpu.get_barrier_semaphore()
    greeted = 0
    for step in range(1, ring):
        pl.semaphore_signal(barrier, inc=1, device_id=xdev(step), device_id_type=MESH)
        pl.semaphore_signal(barrier, inc=1, device_id=ydev(step), device_id_type=MESH)
        greeted += 2
    for step in range(1, experts):
        pl.semaphore_signal(barrier, inc=1, device_id=edev(step), device_id_type=MESH)
        greeted += 1
    for load in loads:
        load.start()
    for load in small:
        load.wait()

    ids, slot = ids_ref[...], slot_ref[...]
    target = jnp.where(slot >= 0, ids * wide + slot, -1)
    place = lax.broadcasted_iota(jnp.int32, (experts * wide, tokens), 0)
    token_hot[...] = jnp.where(place == target, 1.0, 0.0).astype(BF16)
    prob = jnp.broadcast_to(prob_ref[...], (chunk, tokens)).T
    scaled = (prob * grad_ref[...].astype(F32)).astype(BF16)
    bins = jnp.dot(token_hot[...], scaled, preferred_element_type=F32)
    bin_send[...] = bins.astype(BF16).reshape(experts, wide, chunk)

    pl.semaphore_wait(barrier, greeted)

    saved_copies = []
    for step in (2, 1, 3):
        to = lax.rem(mx + step, ring)
        columns = pl.ds(pl.multiple_of((to * ring + my) * chunk, chunk), chunk)
        saved_copies.append(
            remote(saved_ref.at[0, :, columns], saved_recv.at[mx], {"dp": to})
        )
    bin_copies = {}
    for spot, offset in enumerate(OFFSETS):
        if offset != 0:
            to = lax.rem(me + experts - offset, experts)
            bin_copies[spot] = remote(bin_send.at[to], bin_recv.at[spot], {"expert": to})

    lane = lax.broadcasted_iota(jnp.int32, (1, ring * keep), 1)
    position = jnp.full((1, ring * keep), -2, jnp.int32)
    before = jnp.zeros((1, 1), jnp.int32)
    for part in range(ring):
        count = counts_ref[:, part : part + 1]
        inside = (lane >= part * keep) & (lane < part * keep + count)
        position = jnp.where(inside, lane - part * keep + before, position)
        before = before + count
    position = position.astype(F32)
    diagonal = lax.broadcasted_iota(jnp.int32, (cap, cap), 0) == lax.broadcasted_iota(
        jnp.int32, (cap, cap), 1
    )
    for block in range(len(BLOCKS)):
        parts = []
        for spot in range(first_group[block], first_group[block] + BLOCKS[block]):
            group = lax.rem(me + experts + OFFSETS[spot], experts)
            rank = rank_ref[pl.ds(group, 1), :].astype(F32)
            column = jnp.sum(jnp.where(diagonal, rank, 0.0), axis=1, keepdims=True)
            parts.append(jnp.where(column == position, 1.0, 0.0))
        row_hot[span_of(block), :] = jnp.concatenate(parts, axis=0).astype(BF16)

    token_hot_t[...] = token_hot[...].astype(F32).T.astype(BF16)
    for load in loads:
        load.wait()
    w_down_t[...] = w_down[...].astype(F32).T.astype(BF16)
    w_both_t[pl.ds(0, units), :] = w_gate[...].astype(F32).T.astype(BF16)
    w_both_t[pl.ds(units, units), :] = w_up[...].astype(F32).T.astype(BF16)

    x_first, g_first = {}, {}

    def share_x(block):
        span = span_of(block)
        piece = x_all.at[0, my, span]
        steps = (2, 1, 3) if block < DIRECT_SHARES else (1, 3)
        return [remote(piece, x_all.at[ring - step, my, span], xdev(step)) for step in steps]

    def share_g(block):
        span = span_of(block)
        piece = g_all.at[mx, 0, span]
        steps = (2, 1, 3) if block < DIRECT_SHARES else (1, 3)
        return [remote(piece, g_all.at[mx, ring - step, span], ydev(step)) for step in steps]

    def pick_x(block):
        if block == 0:
            for copy in saved_copies:
                copy.wait_recv()
        span = span_of(block)
        x_all[0, my, span, :] = jnp.dot(
            row_hot[span, :], saved_recv[...].reshape(ring * keep, chunk), preferred_element_type=F32
        ).astype(BF16)
        x_first[block] = share_x(block)

    def pick_g(block):
        parts = []
        for spot in range(first_group[block], first_group[block] + BLOCKS[block]):
            if OFFSETS[spot] == 0:
                piece = bin_send[me]
            else:
                bin_copies[spot].wait_recv()
                piece = bin_recv[spot]
            parts.append(piece.astype(F32)[:cap])
        g_all[mx, 0, span_of(block), :] = jnp.concatenate(parts, axis=0).astype(BF16)
        g_first[block] = share_g(block)

    low_x, high_x = lax.rem(mx + ring - 1, ring), lax.rem(mx + 1, ring)
    low_y, high_y = lax.rem(my + ring - 1, ring), lax.rem(my + 1, ring)

    def relay(block):
        if block < DIRECT_SHARES:
            return
        first, second = halves_of(block)
        up, down = x_first[block]
        up.wait_recv()
        sent = [remote(x_all.at[ring - 1, my, first], x_all.at[ring - 2, my, first], xdev(1))]
        down.wait_recv()
        sent.append(remote(x_all.at[1, my, second], x_all.at[2, my, second], xdev(-1)))
        x_first[block] = sent
        up, down = g_first[block]
        up.wait_recv()
        sent = [remote(g_all.at[mx, ring - 1, first], g_all.at[mx, ring - 2, first], ydev(1))]
        down.wait_recv()
        sent.append(remote(g_all.at[mx, 1, second], g_all.at[mx, 2, second], ydev(-1)))
        g_first[block] = sent

    x_own, g_own = [], []

    def two_blocks(part):
        return first_group[2 * part] * cap, sum(BLOCKS[2 * part : 2 * part + 2]) * cap

    def send_own(part, own, piece, cross):
        own.append([remote(piece, piece, cross(1)), remote(piece, piece, cross(-1))])

    def send_own_x(part):
        send_own(part, x_own, x_all.at[0, my, pl.ds(*two_blocks(part))], ydev)

    def send_own_g(part):
        send_own(part, g_own, g_all.at[mx, 0, pl.ds(*two_blocks(part))], xdev)

    def forward_own(part):
        start, size = two_blocks(part)
        cut = size // 32 * 16
        first, second = pl.ds(start, cut), pl.ds(start + cut, size - cut)
        for own, low, high, cross in (
            (x_own, x_all.at[0, low_y, first], x_all.at[0, high_y, second], ydev),
            (g_own, g_all.at[low_x, 0, first], g_all.at[high_x, 0, second], xdev),
        ):
            up, down = own[part]
            up.wait_recv()
            sent = [remote(low, low, cross(1))]
            down.wait_recv()
            sent.append(remote(high, high, cross(-1)))
            own[part] = sent

    near, far = {}, {}
    others = pl.ds(1, ring - 1)

    def spread(block):
        span = span_of(block)
        for copy in x_first[block]:
            copy.wait_recv()
        piece = x_all.at[others, my, span]
        x_near = [remote(piece, piece, ydev(1)), remote(piece, piece, ydev(-1))]
        for copy in g_first[block]:
            copy.wait_recv()
        piece = g_all.at[mx, others, span]
        g_near = [remote(piece, piece, xdev(1)), remote(piece, piece, xdev(-1))]
        near[block] = (x_near, g_near)

    low_half, high_half = pl.ds(0, ring // 2), pl.ds(ring // 2, ring // 2)

    def forward(block):
        span = span_of(block)
        x_near, g_near = near[block]
        first, second = (pl.ds(1, 1), pl.ds(2, 2)) if block % 2 else (pl.ds(1, 2), pl.ds(3, 1))
        x_near[0].wait_recv()
        piece = x_all.at[first, low_y, span]
        copies = [remote(piece, piece, ydev(1))]
        x_near[1].wait_recv()
        piece = x_all.at[second, high_y, span]
        copies.append(remote(piece, piece, ydev(-1)))
        g_near[0].wait_recv()
        piece = g_all.at[low_x, first, span]
        copies.append(remote(piece, piece, xdev(1)))
        g_near[1].wait_recv()
        piece = g_all.at[high_x, second, span]
        copies.append(remote(piece, piece, xdev(-1)))
        far[block] = copies

    def along(which, index, others, span):
        return part_send.at[(index, others, span) if which == 0 else (others, index, span)]

    lines = (
        (xdev, mx, low_x, high_x, ydev, my),
        (ydev, my, low_y, high_y, xdev, mx),
    )
    part_copies, half_copies, back_copies = {}, {}, {}

    def y_place(c):
        return lax.rem(c % ring + ring - my, ring)

    def x_place(c):
        return lax.rem(c // ring + ring - mx, ring)

    def compute(block):
        span = span_of(block)
        if block % 2 == 0:
            for copy in x_own[block // 2] + g_own[block // 2]:
                copy.wait_recv()
        for copy in far[block]:
            copy.wait_recv()
        inputs = jnp.concatenate(
            [x_all[x_place(c), c % ring, span, :] for c in range(ring * ring)], axis=1
        )
        gate_pre = jnp.dot(inputs, w_gate[...], preferred_element_type=F32)
        up_pre = jnp.dot(inputs, w_up[...], preferred_element_type=F32)
        grads = jnp.concatenate(
            [g_all[c // ring, y_place(c), span, :] for c in range(ring * ring)], axis=1
        )
        hidden_grad = jnp.dot(grads, w_down_t[...], preferred_element_type=F32)
        squash = 1.0 / (1.0 + jnp.exp(-gate_pre))
        activated = gate_pre * squash
        hidden_all[span, :] = (activated * up_pre).astype(BF16)
        up_grad = (hidden_grad * activated).astype(BF16)
        gate_grad = (hidden_grad * up_pre * squash * (1.0 + gate_pre * (1.0 - squash))).astype(BF16)
        both_all[span, pl.ds(0, units)] = gate_grad
        both_all[span, pl.ds(units, units)] = up_grad
        both = jnp.concatenate([gate_grad, up_grad], axis=1)
        for x in range(ring):
            piece = pl.ds(x * ring * chunk, ring * chunk)
            total = jnp.dot(both, w_both_t[:, piece], preferred_element_type=F32)
            total = total.astype(BF16)
            for y in range(ring):
                part_send[x, y, span, :] = total[:, y * chunk : (y + 1) * chunk]
        copies = [[], []]
        for which, span in enumerate(halves_of(block, SPLIT)):
            device, mine, low, high = lines[which][:4]
            if block > last - DIRECT_SUMS:
                for step in (2, 1, 3):
                    to = lax.rem(mine + step, ring)
                    copies[which].append(
                        remote(
                            along(which, to, slice(None), span),
                            part_recv.at[step - 1, :, span],
                            device(step),
                        )
                    )
                continue
            other = lax.rem(mine + 2, ring)
            copies[which] = [
                remote(along(which, other, low_half, span), fold_recv.at[0, :, span], device(1)),
                remote(along(which, other, high_half, span), fold_recv.at[1, :, span], device(-1)),
                remote(
                    along(which, high, high_half, span), part_recv.at[0, high_half, span], device(1)
                ),
                remote(
                    along(which, low, low_half, span), part_recv.at[1, low_half, span], device(-1)
                ),
            ]
        part_copies[block] = copies

    def fold(block):
        if block > last - DIRECT_SUMS:
            return
        for which, span in enumerate(halves_of(block, SPLIT)):
            device, mine, low, high = lines[which][:4]
            copies = part_copies[block][which]
            for number, (index, others, step) in enumerate(
                ((high, low_half, 1), (low, high_half, -1))
            ):
                copies[number].wait_recv()
                piece = along(which, index, others, span)
                piece[...] = (
                    piece[...].astype(F32) + fold_recv[number, :, span, :].astype(F32)
                ).astype(BF16)
                copies.append(remote(piece, part_recv.at[number, others, span], device(step)))
            part_copies[block][which] = copies[2:]

    def reduce_first(block):
        sent = [[], []]
        for which, span in enumerate(halves_of(block, SPLIT)):
            mine = lines[which][1]
            device, own = lines[which][4:]
            for copy in part_copies[block][which]:
                copy.wait_recv()
            total = along(which, mine, slice(None), span)[...].astype(F32)
            for step in range(ring - 1 if block > last - DIRECT_SUMS else 2):
                total = total + part_recv[step, :, span, :].astype(F32)
            half_send[:, span, :] = total.astype(BF16)
            for step in (2, 1, 3):
                to = lax.rem(own + step, ring)
                sent[which].append(
                    remote(half_send.at[to, span], half_recv.at[step - 1, span], device(step))
                )
        half_copies[block] = sent

    def reduce_second(block):
        spare = jnp.zeros((wide - cap, chunk), F32)
        totals = []
        for which, span in enumerate(halves_of(block, SPLIT)):
            own = lines[which][5]
            for copy in half_copies[block][which]:
                copy.wait_recv()
            total = half_send[own, span, :].astype(F32)
            for step in range(ring - 1):
                total = total + half_recv[step, span, :].astype(F32)
            totals.append(total)
        total = jnp.concatenate(totals, axis=0)
        for inner in range(BLOCKS[block]):
            spot = first_group[block] + inner
            piece = jnp.concatenate([total[inner * cap : (inner + 1) * cap], spare], axis=0)
            if OFFSETS[spot] == 0:
                back_recv[me] = piece.astype(BF16)
            else:
                back_send[spot] = piece.astype(BF16)
                back_copies[spot] = remote(
                    back_send.at[spot], back_recv.at[me], edev(OFFSETS[spot])
                )

    def weight_grads_in():
        for c in range(ring * ring):
            both = lax.dot_general(
                x_all[x_place(c), c % ring],
                both_all[...],
                (((0,), (0,)), ((), ())),
                preferred_element_type=F32,
            ).astype(BF16)
            dgate_out[0, pl.ds(c * chunk, chunk), :] = both[:, :units]
            dup_out[0, pl.ds(c * chunk, chunk), :] = both[:, units:]

    def weight_grads_out():
        hidden = hidden_all[...].astype(F32).T.astype(BF16)
        for c in range(0, ring * ring, 2):
            pair = jnp.concatenate(
                [g_all[c // ring, y_place(c)], g_all[c // ring, y_place(c + 1)]], axis=1
            )
            ddown_out[0, :, pl.ds(c * chunk, 2 * chunk)] = jnp.dot(
                hidden, pair, preferred_element_type=F32
            ).astype(BF16)

    count = len(BLOCKS)
    pick_g(0)
    pick_g(1)
    send_own_g(0)
    pick_x(0)
    pick_x(1)
    send_own_x(0)
    pick_g(2)
    pick_x(2)
    pick_g(3)
    pick_x(3)
    send_own_x(1)
    send_own_g(1)
    stages = ((relay, -2), (spread, -1), (forward, 0), (compute, 1), (fold, 2), (reduce_first, 3), (reduce_second, 4))
    for turn in range(-2, count + 3):
        if turn == count + 1:
            weight_grads_in()
        if turn == count + 2:
            weight_grads_out()
        if turn in (-1, 0):
            forward_own(turn + 1)
        for stage, lag in stages:
            block = turn - lag
            if stage in (reduce_first, reduce_second):
                if 0 <= block < last:
                    stage(block)
                if block + 1 == last:
                    stage(last)
            elif 0 <= block < count:
                stage(block)

    for copy in back_copies.values():
        copy.wait_recv()
    returned = back_recv[...].reshape(experts * wide, chunk)
    dinput_out[...] = jnp.dot(token_hot_t[...], returned, preferred_element_type=F32).astype(BF16)
    for copy in started:
        copy.wait_send()


def write_out(*refs):
    sources, targets, sem = refs[:4], refs[4:8], refs[8]
    copies = []
    for source, target in zip(sources, targets):
        if len(source.shape) == 2:
            copies.append((source, target))
        else:
            size = source.shape[1] // 4
            for part in range(4):
                piece = pl.ds(part * size, size)
                copies.append((source.at[:, piece], target.at[:, piece]))
    copies = [
        pltpu.make_async_copy(source, target, sem.at[number])
        for number, (source, target) in enumerate(copies)
    ]
    for copy in copies:
        copy.start()
    for copy in copies:
        copy.wait()


def local(
    grad_out,
    gate_prob,
    expert_ids,
    slot_index,
    saved_rows,
    row_rank,
    part_counts,
    w_gate,
    w_up,
    w_down,
):
    experts, cap = row_rank.shape[1], row_rank.shape[2]
    tokens, chunk = grad_out.shape
    ring = part_counts.shape[1]
    keep = saved_rows.shape[1]
    width, units = w_gate.shape[1], w_gate.shape[2]
    slots = experts * cap
    wide = 48
    copies = 2 * (experts - 1) + 3 + len(BLOCKS) * (8 + 8 + 12 + 6) + 16
    vmem = pl.BlockSpec(memory_space=pltpu.VMEM)
    anywhere = pl.BlockSpec(memory_space=pl.ANY)
    held = pl.pallas_call(
        functools.partial(kernel, cap),
        out_shape=(
            pltpu.VMEM((tokens, chunk), BF16),
            pltpu.VMEM(w_gate.shape, BF16),
            pltpu.VMEM(w_up.shape, BF16),
            pltpu.VMEM(w_down.shape, BF16),
        ),
        in_specs=[anywhere] * 10,
        out_specs=(vmem,) * 4,
        scratch_shapes=[
            pltpu.VMEM((tokens, chunk), BF16),
            pltpu.VMEM((1, tokens), F32),
            pltpu.VMEM((1, tokens), jnp.int32),
            pltpu.VMEM((1, tokens), jnp.int32),
            pltpu.VMEM((experts, cap), jnp.int32),
            pltpu.VMEM((1, ring), jnp.int32),
            pltpu.VMEM((width, units), BF16),
            pltpu.VMEM((width, units), BF16),
            pltpu.VMEM((units, width), BF16),
            pltpu.VMEM((experts * wide, tokens), BF16),
            pltpu.VMEM((tokens, experts * wide), BF16),
            pltpu.VMEM((width, units), BF16),
            pltpu.VMEM((2 * units, width), BF16),
            pltpu.VMEM((slots, ring * keep), BF16),
            pltpu.VMEM((experts, wide, chunk), BF16),
            pltpu.VMEM((experts, wide, chunk), BF16),
            pltpu.VMEM((ring, keep, chunk), BF16),
            pltpu.VMEM((ring, ring, slots, chunk), BF16),
            pltpu.VMEM((ring, ring, slots, chunk), BF16),
            pltpu.VMEM((slots, units), BF16),
            pltpu.VMEM((slots, 2 * units), BF16),
            pltpu.VMEM((ring, ring, slots, chunk), BF16),
            pltpu.VMEM((2, ring // 2, slots, chunk), BF16),
            pltpu.VMEM((ring - 1, ring, slots, chunk), BF16),
            pltpu.VMEM((ring, slots, chunk), BF16),
            pltpu.VMEM((ring - 1, slots, chunk), BF16),
            pltpu.VMEM((experts, wide, chunk), BF16),
            pltpu.VMEM((experts, wide, chunk), BF16),
            pltpu.SemaphoreType.DMA((10,)),
            pltpu.SemaphoreType.DMA((copies,)),
            pltpu.SemaphoreType.DMA((copies,)),
        ],
        compiler_params=pltpu.CompilerParams(
            collective_id=0, has_side_effects=True, vmem_limit_bytes=52 << 20
        ),
        name="experts_backward",
    )(
        grad_out,
        gate_prob.reshape(1, tokens),
        expert_ids.reshape(1, tokens),
        slot_index.reshape(1, tokens),
        saved_rows,
        row_rank,
        part_counts,
        w_gate,
        w_up,
        w_down,
    )
    held = [pltpu.with_memory_space_constraint(part, pltpu.VMEM) for part in held]
    return pl.pallas_call(
        write_out,
        out_shape=tuple(jax.ShapeDtypeStruct(part.shape, part.dtype) for part in held),
        in_specs=[vmem] * 4,
        out_specs=(anywhere,) * 4,
        scratch_shapes=[pltpu.SemaphoreType.DMA((13,))],
        name="write_out",
    )(*held)


def solution(mesh):
    placed = (
        P("expert", ("dp", "tensor")),
        P("expert"),
        P("expert"),
        P("expert"),
        P("expert", "dp", None),
        P("expert", None, None),
        P("expert", None),
        P("expert", None, ("dp", "tensor")),
        P("expert", None, ("dp", "tensor")),
        P("expert", ("dp", "tensor"), None),
    )
    return jax.shard_map(
        local,
        mesh=mesh,
        in_specs=placed,
        out_specs=(
            P("expert", ("dp", "tensor")),
            P("expert", None, ("dp", "tensor")),
            P("expert", None, ("dp", "tensor")),
            P("expert", ("dp", "tensor"), None),
        ),
        check_vma=False,
    )
```

```python
import functools

import jax
import jax.numpy as jnp
from jax import lax
from jax.experimental import pallas as pl
from jax.experimental.pallas import tpu as pltpu
from jax.sharding import PartitionSpec as P

MESH = pl.DeviceIdType.MESH
BF16, F32 = jnp.bfloat16, jnp.float32
BLOCKS = (4, 4, 4, 4)
DIRECT_SHARES = 1
DIRECT_SUMS = 1
SPLIT = 2.5
OFFSETS = (-2, 3, -3, 4, -4, 5, -5, 6, -6, 7, -7, 8, 0, 1, -1, 2)


def kernel(
    cap,
    grad_hbm,
    prob_hbm,
    ids_hbm,
    slot_hbm,
    saved_ref,
    rank_hbm,
    counts_hbm,
    gate_hbm,
    up_hbm,
    down_hbm,
    dinput_out,
    dgate_out,
    dup_out,
    ddown_out,
    grad_ref,
    prob_ref,
    ids_ref,
    slot_ref,
    rank_ref,
    counts_ref,
    w_gate,
    w_up,
    w_down,
    token_hot,
    token_hot_t,
    w_down_t,
    w_both_t,
    row_hot,
    bin_send,
    bin_recv,
    saved_recv,
    x_all,
    g_all,
    hidden_all,
    both_all,
    part_send,
    fold_recv,
    part_recv,
    half_send,
    half_recv,
    back_send,
    back_recv,
    local_sem,
    send_sem,
    recv_sem,
):
    experts = lax.axis_size("expert")
    me, mx, my = lax.axis_index("expert"), lax.axis_index("dp"), lax.axis_index("tensor")
    ring = lax.axis_size("dp")
    keep = saved_ref.shape[1]
    wide = bin_send.shape[1]
    tokens, chunk = grad_ref.shape
    units = w_gate.shape[1]
    last = len(BLOCKS) - 1
    first_group = [sum(BLOCKS[:block]) for block in range(len(BLOCKS))]

    def rows_of(block):
        return first_group[block] * cap, BLOCKS[block] * cap

    def span_of(block):
        return pl.ds(*rows_of(block))

    def halves_of(block, share=2.5):
        start, size = rows_of(block)
        cut = int(size * share / 5) // 16 * 16
        return (pl.ds(start, cut), pl.ds(start + cut, size - cut))

    started = []

    def remote(src, dst, device):
        number = len(started)
        copy = pltpu.make_async_remote_copy(
            src_ref=src,
            dst_ref=dst,
            send_sem=send_sem.at[number],
            recv_sem=recv_sem.at[number],
            device_id=device,
            device_id_type=MESH,
        )
        copy.start()
        started.append(copy)
        return copy

    def xdev(step):
        return {"dp": lax.rem(mx + ring + step, ring)}

    def ydev(step):
        return {"tensor": lax.rem(my + ring + step, ring)}

    def edev(step):
        return {"expert": lax.rem(me + experts + step, experts)}

    small = [
        pltpu.make_async_copy(src, dst, local_sem.at[number])
        for number, (src, dst) in enumerate(
            (
                (grad_hbm, grad_ref),
                (prob_hbm, prob_ref),
                (ids_hbm, ids_ref),
                (slot_hbm, slot_ref),
                (rank_hbm.at[0], rank_ref),
                (counts_hbm, counts_ref),
                (
                    saved_ref.at[0, :, pl.ds(pl.multiple_of((mx * ring + my) * chunk, chunk), chunk)],
                    saved_recv.at[mx],
                ),
            )
        )
    ]
    loads = [
        pltpu.make_async_copy(src.at[0], dst, local_sem.at[len(small) + number])
        for number, (src, dst) in enumerate(((gate_hbm, w_gate), (up_hbm, w_up), (down_hbm, w_down)))
    ]
    for load in small:
        load.start()

    barrier = pltpu.get_barrier_semaphore()
    greeted = 0
    for step in range(1, ring):
        pl.semaphore_signal(barrier, inc=1, device_id=xdev(step), device_id_type=MESH)
        pl.semaphore_signal(barrier, inc=1, device_id=ydev(step), device_id_type=MESH)
        greeted += 2
    for step in range(1, experts):
        pl.semaphore_signal(barrier, inc=1, device_id=edev(step), device_id_type=MESH)
        greeted += 1
    for load in loads:
        load.start()
    for load in small:
        load.wait()

    ids, slot = ids_ref[...], slot_ref[...]
    target = jnp.where(slot >= 0, ids * wide + slot, -1)
    place = lax.broadcasted_iota(jnp.int32, (experts * wide, tokens), 0)
    token_hot[...] = jnp.where(place == target, 1.0, 0.0).astype(BF16)
    prob = jnp.broadcast_to(prob_ref[...], (chunk, tokens)).T
    scaled = (prob * grad_ref[...].astype(F32)).astype(BF16)
    bins = jnp.dot(token_hot[...], scaled, preferred_element_type=F32)
    bin_send[...] = bins.astype(BF16).reshape(experts, wide, chunk)

    pl.semaphore_wait(barrier, greeted)

    saved_copies = []
    for step in (2, 1, 3):
        to = lax.rem(mx + step, ring)
        columns = pl.ds(pl.multiple_of((to * ring + my) * chunk, chunk), chunk)
        saved_copies.append(
            remote(saved_ref.at[0, :, columns], saved_recv.at[mx], {"dp": to})
        )
    bin_copies = {}
    for spot, offset in enumerate(OFFSETS):
        if offset != 0:
            to = lax.rem(me + experts - offset, experts)
            bin_copies[spot] = remote(bin_send.at[to], bin_recv.at[spot], {"expert": to})

    lane = lax.broadcasted_iota(jnp.int32, (1, ring * keep), 1)
    position = jnp.full((1, ring * keep), -2, jnp.int32)
    before = jnp.zeros((1, 1), jnp.int32)
    for part in range(ring):
        count = counts_ref[:, part : part + 1]
        inside = (lane >= part * keep) & (lane < part * keep + count)
        position = jnp.where(inside, lane - part * keep + before, position)
        before = before + count
    position = position.astype(F32)
    diagonal = lax.broadcasted_iota(jnp.int32, (cap, cap), 0) == lax.broadcasted_iota(
        jnp.int32, (cap, cap), 1
    )
    for block in range(len(BLOCKS)):
        parts = []
        for spot in range(first_group[block], first_group[block] + BLOCKS[block]):
            group = lax.rem(me + experts + OFFSETS[spot], experts)
            rank = rank_ref[pl.ds(group, 1), :].astype(F32)
            column = jnp.sum(jnp.where(diagonal, rank, 0.0), axis=1, keepdims=True)
            parts.append(jnp.where(column == position, 1.0, 0.0))
        row_hot[span_of(block), :] = jnp.concatenate(parts, axis=0).astype(BF16)

    token_hot_t[...] = token_hot[...].astype(F32).T.astype(BF16)
    for load in loads:
        load.wait()
    w_down_t[...] = w_down[...].astype(F32).T.astype(BF16)
    w_both_t[pl.ds(0, units), :] = w_gate[...].astype(F32).T.astype(BF16)
    w_both_t[pl.ds(units, units), :] = w_up[...].astype(F32).T.astype(BF16)

    x_first, g_first = {}, {}

    def share_x(block):
        span = span_of(block)
        piece = x_all.at[0, my, span]
        steps = (2, 1, 3) if block < DIRECT_SHARES else (1, 3)
        return [remote(piece, x_all.at[ring - step, my, span], xdev(step)) for step in steps]

    def share_g(block):
        span = span_of(block)
        piece = g_all.at[mx, 0, span]
        steps = (2, 1, 3) if block < DIRECT_SHARES else (1, 3)
        return [remote(piece, g_all.at[mx, ring - step, span], ydev(step)) for step in steps]

    def pick_x(block):
        if block == 0:
            for copy in saved_copies:
                copy.wait_recv()
        span = span_of(block)
        x_all[0, my, span, :] = jnp.dot(
            row_hot[span, :], saved_recv[...].reshape(ring * keep, chunk), preferred_element_type=F32
        ).astype(BF16)
        x_first[block] = share_x(block)

    def pick_g(block):
        parts = []
        for spot in range(first_group[block], first_group[block] + BLOCKS[block]):
            if OFFSETS[spot] == 0:
                piece = bin_send[me]
            else:
                bin_copies[spot].wait_recv()
                piece = bin_recv[spot]
            parts.append(piece.astype(F32)[:cap])
        g_all[mx, 0, span_of(block), :] = jnp.concatenate(parts, axis=0).astype(BF16)
        g_first[block] = share_g(block)

    low_x, high_x = lax.rem(mx + ring - 1, ring), lax.rem(mx + 1, ring)
    low_y, high_y = lax.rem(my + ring - 1, ring), lax.rem(my + 1, ring)

    def relay(block):
        if block < DIRECT_SHARES:
            return
        first, second = halves_of(block)
        up, down = x_first[block]
        up.wait_recv()
        sent = [remote(x_all.at[ring - 1, my, first], x_all.at[ring - 2, my, first], xdev(1))]
        down.wait_recv()
        sent.append(remote(x_all.at[1, my, second], x_all.at[2, my, second], xdev(-1)))
        x_first[block] = sent
        up, down = g_first[block]
        up.wait_recv()
        sent = [remote(g_all.at[mx, ring - 1, first], g_all.at[mx, ring - 2, first], ydev(1))]
        down.wait_recv()
        sent.append(remote(g_all.at[mx, 1, second], g_all.at[mx, 2, second], ydev(-1)))
        g_first[block] = sent

    x_own, g_own = [], []

    def two_blocks(part):
        return first_group[2 * part] * cap, sum(BLOCKS[2 * part : 2 * part + 2]) * cap

    def send_own(part, own, piece, cross):
        own.append([remote(piece, piece, cross(1)), remote(piece, piece, cross(-1))])

    def send_own_x(part):
        send_own(part, x_own, x_all.at[0, my, pl.ds(*two_blocks(part))], ydev)

    def send_own_g(part):
        send_own(part, g_own, g_all.at[mx, 0, pl.ds(*two_blocks(part))], xdev)

    def forward_own(part):
        start, size = two_blocks(part)
        cut = size // 32 * 16
        first, second = pl.ds(start, cut), pl.ds(start + cut, size - cut)
        for own, low, high, cross in (
            (x_own, x_all.at[0, low_y, first], x_all.at[0, high_y, second], ydev),
            (g_own, g_all.at[low_x, 0, first], g_all.at[high_x, 0, second], xdev),
        ):
            up, down = own[part]
            up.wait_recv()
            sent = [remote(low, low, cross(1))]
            down.wait_recv()
            sent.append(remote(high, high, cross(-1)))
            own[part] = sent

    near, far = {}, {}
    others = pl.ds(1, ring - 1)

    def spread(block):
        span = span_of(block)
        for copy in x_first[block]:
            copy.wait_recv()
        piece = x_all.at[others, my, span]
        x_near = [remote(piece, piece, ydev(1)), remote(piece, piece, ydev(-1))]
        for copy in g_first[block]:
            copy.wait_recv()
        piece = g_all.at[mx, others, span]
        g_near = [remote(piece, piece, xdev(1)), remote(piece, piece, xdev(-1))]
        near[block] = (x_near, g_near)

    low_half, high_half = pl.ds(0, ring // 2), pl.ds(ring // 2, ring // 2)

    def forward(block):
        span = span_of(block)
        x_near, g_near = near[block]
        first, second = (pl.ds(1, 1), pl.ds(2, 2)) if block % 2 else (pl.ds(1, 2), pl.ds(3, 1))
        x_near[0].wait_recv()
        piece = x_all.at[first, low_y, span]
        copies = [remote(piece, piece, ydev(1))]
        x_near[1].wait_recv()
        piece = x_all.at[second, high_y, span]
        copies.append(remote(piece, piece, ydev(-1)))
        g_near[0].wait_recv()
        piece = g_all.at[low_x, first, span]
        copies.append(remote(piece, piece, xdev(1)))
        g_near[1].wait_recv()
        piece = g_all.at[high_x, second, span]
        copies.append(remote(piece, piece, xdev(-1)))
        far[block] = copies

    def along(which, index, others, span):
        return part_send.at[(index, others, span) if which == 0 else (others, index, span)]

    lines = (
        (xdev, mx, low_x, high_x, ydev, my),
        (ydev, my, low_y, high_y, xdev, mx),
    )
    part_copies, half_copies, back_copies = {}, {}, {}

    def y_place(c):
        return lax.rem(c % ring + ring - my, ring)

    def x_place(c):
        return lax.rem(c // ring + ring - mx, ring)

    def compute(block):
        span = span_of(block)
        if block % 2 == 0:
            for copy in x_own[block // 2] + g_own[block // 2]:
                copy.wait_recv()
        for copy in far[block]:
            copy.wait_recv()
        inputs = jnp.concatenate(
            [x_all[x_place(c), c % ring, span, :] for c in range(ring * ring)], axis=1
        )
        gate_pre = jnp.dot(inputs, w_gate[...], preferred_element_type=F32)
        up_pre = jnp.dot(inputs, w_up[...], preferred_element_type=F32)
        grads = jnp.concatenate(
            [g_all[c // ring, y_place(c), span, :] for c in range(ring * ring)], axis=1
        )
        hidden_grad = jnp.dot(grads, w_down_t[...], preferred_element_type=F32)
        squash = 1.0 / (1.0 + jnp.exp(-gate_pre))
        activated = gate_pre * squash
        hidden_all[span, :] = (activated * up_pre).astype(BF16)
        up_grad = (hidden_grad * activated).astype(BF16)
        gate_grad = (hidden_grad * up_pre * squash * (1.0 + gate_pre * (1.0 - squash))).astype(BF16)
        both_all[span, pl.ds(0, units)] = gate_grad
        both_all[span, pl.ds(units, units)] = up_grad
        both = jnp.concatenate([gate_grad, up_grad], axis=1)
        for x in range(ring):
            piece = pl.ds(x * ring * chunk, ring * chunk)
            total = jnp.dot(both, w_both_t[:, piece], preferred_element_type=F32)
            total = total.astype(BF16)
            for y in range(ring):
                part_send[x, y, span, :] = total[:, y * chunk : (y + 1) * chunk]
        copies = [[], []]
        for which, span in enumerate(halves_of(block, SPLIT)):
            device, mine, low, high = lines[which][:4]
            if block > last - DIRECT_SUMS:
                for step in (2, 1, 3):
                    to = lax.rem(mine + step, ring)
                    copies[which].append(
                        remote(
                            along(which, to, slice(None), span),
                            part_recv.at[step - 1, :, span],
                            device(step),
                        )
                    )
                continue
            other = lax.rem(mine + 2, ring)
            copies[which] = [
                remote(along(which, other, low_half, span), fold_recv.at[0, :, span], device(1)),
                remote(along(which, other, high_half, span), fold_recv.at[1, :, span], device(-1)),
                remote(
                    along(which, high, high_half, span), part_recv.at[0, high_half, span], device(1)
                ),
                remote(
                    along(which, low, low_half, span), part_recv.at[1, low_half, span], device(-1)
                ),
            ]
        part_copies[block] = copies

    def fold(block):
        if block > last - DIRECT_SUMS:
            return
        for which, span in enumerate(halves_of(block, SPLIT)):
            device, mine, low, high = lines[which][:4]
            copies = part_copies[block][which]
            for number, (index, others, step) in enumerate(
                ((high, low_half, 1), (low, high_half, -1))
            ):
                copies[number].wait_recv()
                piece = along(which, index, others, span)
                piece[...] = (
                    piece[...].astype(F32) + fold_recv[number, :, span, :].astype(F32)
                ).astype(BF16)
                copies.append(remote(piece, part_recv.at[number, others, span], device(step)))
            part_copies[block][which] = copies[2:]

    def reduce_first(block):
        sent = [[], []]
        for which, span in enumerate(halves_of(block, SPLIT)):
            mine = lines[which][1]
            device, own = lines[which][4:]
            for copy in part_copies[block][which]:
                copy.wait_recv()
            total = along(which, mine, slice(None), span)[...].astype(F32)
            for step in range(ring - 1 if block > last - DIRECT_SUMS else 2):
                total = total + part_recv[step, :, span, :].astype(F32)
            half_send[:, span, :] = total.astype(BF16)
            for step in (2, 1, 3):
                to = lax.rem(own + step, ring)
                sent[which].append(
                    remote(half_send.at[to, span], half_recv.at[step - 1, span], device(step))
                )
        half_copies[block] = sent

    def reduce_second(block):
        spare = jnp.zeros((wide - cap, chunk), F32)
        totals = []
        for which, span in enumerate(halves_of(block, SPLIT)):
            own = lines[which][5]
            for copy in half_copies[block][which]:
                copy.wait_recv()
            total = half_send[own, span, :].astype(F32)
            for step in range(ring - 1):
                total = total + half_recv[step, span, :].astype(F32)
            totals.append(total)
        total = jnp.concatenate(totals, axis=0)
        for inner in range(BLOCKS[block]):
            spot = first_group[block] + inner
            piece = jnp.concatenate([total[inner * cap : (inner + 1) * cap], spare], axis=0)
            if OFFSETS[spot] == 0:
                back_recv[me] = piece.astype(BF16)
            else:
                back_send[spot] = piece.astype(BF16)
                back_copies[spot] = remote(
                    back_send.at[spot], back_recv.at[me], edev(OFFSETS[spot])
                )

    def weight_grads_in():
        for c in range(ring * ring):
            both = lax.dot_general(
                x_all[x_place(c), c % ring],
                both_all[...],
                (((0,), (0,)), ((), ())),
                preferred_element_type=F32,
            ).astype(BF16)
            dgate_out[0, pl.ds(c * chunk, chunk), :] = both[:, :units]
            dup_out[0, pl.ds(c * chunk, chunk), :] = both[:, units:]

    def weight_grads_out():
        hidden = hidden_all[...].astype(F32).T.astype(BF16)
        for c in range(0, ring * ring, 2):
            pair = jnp.concatenate(
                [g_all[c // ring, y_place(c)], g_all[c // ring, y_place(c + 1)]], axis=1
            )
            ddown_out[0, :, pl.ds(c * chunk, 2 * chunk)] = jnp.dot(
                hidden, pair, preferred_element_type=F32
            ).astype(BF16)

    count = len(BLOCKS)
    pick_g(0)
    pick_g(1)
    send_own_g(0)
    pick_x(0)
    pick_x(1)
    send_own_x(0)
    pick_g(2)
    pick_x(2)
    pick_g(3)
    pick_x(3)
    send_own_x(1)
    send_own_g(1)
    stages = ((relay, -2), (spread, -1), (forward, 0), (compute, 1), (fold, 2), (reduce_first, 3), (reduce_second, 4))
    for turn in range(-2, count):
        if turn in (-1, 0):
            forward_own(turn + 1)
        for stage, lag in stages:
            if 0 <= turn - lag < count:
                stage(turn - lag)
    compute(last)
    fold(last - 1)
    reduce_first(last - 2)
    reduce_second(last - 3)
    weight_grads_in()
    reduce_first(last - 1)
    reduce_second(last - 2)
    reduce_first(last)
    reduce_second(last - 1)
    weight_grads_out()
    reduce_second(last)

    for copy in back_copies.values():
        copy.wait_recv()
    returned = back_recv[...].reshape(experts * wide, chunk)
    dinput_out[...] = jnp.dot(token_hot_t[...], returned, preferred_element_type=F32).astype(BF16)
    for copy in started:
        copy.wait_send()


def write_out(*refs):
    sources, targets, sem = refs[:4], refs[4:8], refs[8]
    copies = []
    for source, target in zip(sources, targets):
        if len(source.shape) == 2:
            copies.append((source, target))
        else:
            size = source.shape[1] // 4
            for part in range(4):
                piece = pl.ds(part * size, size)
                copies.append((source.at[:, piece], target.at[:, piece]))
    copies = [
        pltpu.make_async_copy(source, target, sem.at[number])
        for number, (source, target) in enumerate(copies)
    ]
    for copy in copies:
        copy.start()
    for copy in copies:
        copy.wait()


def local(
    grad_out,
    gate_prob,
    expert_ids,
    slot_index,
    saved_rows,
    row_rank,
    part_counts,
    w_gate,
    w_up,
    w_down,
):
    experts, cap = row_rank.shape[1], row_rank.shape[2]
    tokens, chunk = grad_out.shape
    ring = part_counts.shape[1]
    keep = saved_rows.shape[1]
    width, units = w_gate.shape[1], w_gate.shape[2]
    slots = experts * cap
    wide = 48
    copies = 2 * (experts - 1) + 3 + len(BLOCKS) * (8 + 8 + 12 + 6) + 16
    vmem = pl.BlockSpec(memory_space=pltpu.VMEM)
    anywhere = pl.BlockSpec(memory_space=pl.ANY)
    held = pl.pallas_call(
        functools.partial(kernel, cap),
        out_shape=(
            pltpu.VMEM((tokens, chunk), BF16),
            pltpu.VMEM(w_gate.shape, BF16),
            pltpu.VMEM(w_up.shape, BF16),
            pltpu.VMEM(w_down.shape, BF16),
        ),
        in_specs=[anywhere] * 10,
        out_specs=(vmem,) * 4,
        scratch_shapes=[
            pltpu.VMEM((tokens, chunk), BF16),
            pltpu.VMEM((1, tokens), F32),
            pltpu.VMEM((1, tokens), jnp.int32),
            pltpu.VMEM((1, tokens), jnp.int32),
            pltpu.VMEM((experts, cap), jnp.int32),
            pltpu.VMEM((1, ring), jnp.int32),
            pltpu.VMEM((width, units), BF16),
            pltpu.VMEM((width, units), BF16),
            pltpu.VMEM((units, width), BF16),
            pltpu.VMEM((experts * wide, tokens), BF16),
            pltpu.VMEM((tokens, experts * wide), BF16),
            pltpu.VMEM((width, units), BF16),
            pltpu.VMEM((2 * units, width), BF16),
            pltpu.VMEM((slots, ring * keep), BF16),
            pltpu.VMEM((experts, wide, chunk), BF16),
            pltpu.VMEM((experts, wide, chunk), BF16),
            pltpu.VMEM((ring, keep, chunk), BF16),
            pltpu.VMEM((ring, ring, slots, chunk), BF16),
            pltpu.VMEM((ring, ring, slots, chunk), BF16),
            pltpu.VMEM((slots, units), BF16),
            pltpu.VMEM((slots, 2 * units), BF16),
            pltpu.VMEM((ring, ring, slots, chunk), BF16),
            pltpu.VMEM((2, ring // 2, slots, chunk), BF16),
            pltpu.VMEM((ring - 1, ring, slots, chunk), BF16),
            pltpu.VMEM((ring, slots, chunk), BF16),
            pltpu.VMEM((ring - 1, slots, chunk), BF16),
            pltpu.VMEM((experts, wide, chunk), BF16),
            pltpu.VMEM((experts, wide, chunk), BF16),
            pltpu.SemaphoreType.DMA((10,)),
            pltpu.SemaphoreType.DMA((copies,)),
            pltpu.SemaphoreType.DMA((copies,)),
        ],
        compiler_params=pltpu.CompilerParams(
            collective_id=0, has_side_effects=True, vmem_limit_bytes=52 << 20
        ),
        name="experts_backward",
    )(
        grad_out,
        gate_prob.reshape(1, tokens),
        expert_ids.reshape(1, tokens),
        slot_index.reshape(1, tokens),
        saved_rows,
        row_rank,
        part_counts,
        w_gate,
        w_up,
        w_down,
    )
    held = [pltpu.with_memory_space_constraint(part, pltpu.VMEM) for part in held]
    return pl.pallas_call(
        write_out,
        out_shape=tuple(jax.ShapeDtypeStruct(part.shape, part.dtype) for part in held),
        in_specs=[vmem] * 4,
        out_specs=(anywhere,) * 4,
        scratch_shapes=[pltpu.SemaphoreType.DMA((13,))],
        name="write_out",
    )(*held)


def solution(mesh):
    placed = (
        P("expert", ("dp", "tensor")),
        P("expert"),
        P("expert"),
        P("expert"),
        P("expert", "dp", None),
        P("expert", None, None),
        P("expert", None),
        P("expert", None, ("dp", "tensor")),
        P("expert", None, ("dp", "tensor")),
        P("expert", ("dp", "tensor"), None),
    )
    return jax.shard_map(
        local,
        mesh=mesh,
        in_specs=placed,
        out_specs=(
            P("expert", ("dp", "tensor")),
            P("expert", None, ("dp", "tensor")),
            P("expert", None, ("dp", "tensor")),
            P("expert", ("dp", "tensor"), None),
        ),
        check_vma=False,
    )
```
